256 devices in a mesh: seq: 32 (over y, x, core), exp: 8 (over z).
Axes of the slice: x: 4, y: 4, z: 8, core: 2. Of those that a mesh axis runs over, the one named last changes fastest.
Arguments:
- queries: bfloat16 [32768, 2048], P('seq', 'exp'), may hold values from -6 to 6
- keys: bfloat16 [32768, 2048], P('seq', 'exp'), may hold values from -6 to 6
- values: bfloat16 [32768, 2048], P('seq', 'exp'), may hold values from -6 to 6
- out_gate: bfloat16 [32768, 2048], P('seq', 'exp'), may hold values from -6 to 6
- decay_log: float32 [32768, 2048], P('seq', 'exp'), may hold values from -0.86 to 0
- beta: float32 [16, 32768], P('exp', 'seq'), may hold values from 0.0005 to 0.98
- w_out: bfloat16 [2048, 1152], P('exp'), may hold values from -0.125 to 0.125
- resid: bfloat16 [32768, 1152], P(('seq', 'exp')), may hold values from -6 to 6
- norm_gain: float32 [1152], replicated, may hold values from 0.1 to 1.9
- router: bfloat16 [1152, 256], replicated, may hold values from -0.1875 to 0.1875
- w_gate_up: bfloat16 [256, 1152, 2048], P(('seq', 'exp')), may hold values from -0.1875 to 0.1875
- w_down: bfloat16 [256, 1024, 1152], P(('seq', 'exp')), may hold values from -0.1875 to 0.1875
- block_experts: int32 [256, 8], replicated, may hold values from 0 to 255, as said below
Outputs:
- moe_out: bfloat16 [32768, 1152], P(('seq', 'exp'))
The draws below stay inside these ranges and needn't reach their ends.
Inputs may be any that keep to these rules, and one draw needn't show every extreme that they name: `block_experts`: expert e is counted as row e // 8 and column e % 8; slot j of every block names an expert of column j % 8. `block_experts`: for every seq index s and column c, the 8 slots of column c in blocks s * 8 to s * 8 + 7 name experts of 8 different rows. `block_experts`: every expert is named by 1 to 14 slots of the whole batch, and some expert by exactly 14.
All inputs are finite; a program needn't handle non-finite values.
Results may differ from the reference program's by a relative error of at most 0.023.
Values may be sent and summed in bfloat16 or wider, within the bound.
A program may use at most 128 MiB of HBM per device.

```python
import jax
import jax.numpy as jnp
from jax import lax

D = 1152
HEADS = 16
DK = 128
FF = 1024
TOPK = 8
TOK_DEV = 128
TOK_SEQ = 1024
TOKEN_COUNT = 32768
BLOCKS = 256
EXPERTS = 256


def draw_decay_log(key, part):
    key = jax.random.fold_in(key, 11)
    every_key_row = jax.random.split(key, 7)
    channel_width = HEADS * DK
    fast_share = 0.5
    fast_mask = jax.random.bernoulli(every_key_row[0], fast_share, (channel_width,))
    fast_rate = jax.random.uniform(every_key_row[1], (channel_width,), jnp.float32, 2.3 / 50.0, 2.3 / 30.0)
    slow_rate = jax.random.uniform(every_key_row[2], (channel_width,), jnp.float32, 0.05, 0.5) / TOKEN_COUNT
    decay_rate = jnp.where(fast_mask, fast_rate, slow_rate)
    groups = TOKEN_COUNT // TOK_SEQ
    spread = jax.random.uniform(every_key_row[3], (groups, 1, channel_width), jnp.float32, 0.6, 1.4)
    roughness = jax.random.uniform(every_key_row[4], (groups, TOK_SEQ, channel_width), jnp.float32, 0.5, 1.5)
    constant_level = -(decay_rate * roughness * spread).reshape(TOKEN_COUNT, channel_width)
    spike_positions = jax.random.randint(every_key_row[5], (2,), 0, TOKEN_COUNT)
    hit_positions = jnp.any(jnp.arange(TOKEN_COUNT)[:, None] == spike_positions[None, :], axis=1)
    spike_loss_value = jnp.log(jax.random.uniform(every_key_row[6], (TOKEN_COUNT, channel_width), jnp.float32, 0.5, 0.8))
    return constant_level + jnp.where(hit_positions[:, None], spike_loss_value, 0.0)


def draw_beta(key, part):
    key = jax.random.fold_in(key, 37)
    every_key_row = jax.random.split(key, 3)
    writing_count = max(1, HEADS // 2)
    logits = jnp.clip(1.5 * jax.random.normal(every_key_row[1], (HEADS, TOKEN_COUNT), jnp.float32), -3.8, 3.8)
    head_rank = jax.random.permutation(every_key_row[0], HEADS)
    writing = head_rank < writing_count
    strong = jax.nn.sigmoid(logits)
    weak = jnp.exp(jax.random.uniform(every_key_row[2], (HEADS, TOKEN_COUNT), jnp.float32, jnp.log(0.00051), jnp.log(0.005)))
    return jnp.where(writing[:, None], strong, weak)


def draw_block_experts(key, part):
    key = jax.random.fold_in(key, 23)
    seq_count = TOKEN_COUNT // TOK_SEQ
    exp_count = TOK_SEQ // TOK_DEV
    per_column = TOPK // exp_count
    half_rows = seq_count // 2
    hot_picks = min(TOPK - 1, half_rows)
    cold_picks = TOPK - hot_picks

    def column_rows(column_key):
        keys_col = jax.random.split(column_key, 3)
        row_order = jax.random.permutation(keys_col[0], seq_count)
        source_order = jax.random.permutation(keys_col[1], seq_count)
        hot_index = (source_order[:, None] * hot_picks + jnp.arange(hot_picks)[None, :]) % half_rows
        cold_index = (source_order[:, None] * cold_picks + jnp.arange(cold_picks)[None, :]) % half_rows + half_rows
        chosen = jnp.take(row_order, jnp.concatenate([hot_index, cold_index], axis=1))
        noise = jax.random.randint(keys_col[2], (seq_count, TOPK), 0, 1 << 20) * TOPK + jnp.arange(TOPK)[None, :]
        shuffle = jnp.argsort(noise, axis=1, stable=True)
        return jnp.take_along_axis(chosen, shuffle, axis=1)
    rows_all = jax.vmap(column_rows)(jax.random.split(key, exp_count))
    numbers = rows_all * exp_count + jnp.arange(exp_count)[:, None, None]
    arranged = jnp.transpose(numbers.reshape(exp_count, seq_count, exp_count, per_column), (1, 2, 3, 0))
    return arranged.reshape(seq_count * exp_count, TOPK).astype(jnp.int32)


def steps_of(key, extent, pieces, least, top_value):
    level, own = 1.0, jax.random.fold_in(key, 6)
    for dim, shards_of in pieces:
        heights = jnp.exp(jax.random.uniform(jax.random.fold_in(own, dim), (shards_of,), jnp.float32, least / len(pieces), top_value / len(pieces)))
        level = level * jnp.repeat(heights, extent[dim] // shards_of).reshape([-1 if axis == dim else 1 for axis in range(len(extent))])
    return level


def normal_values(rng, dims, width, bound, shards=(), held_as=jnp.bfloat16):
    values = width * jax.random.normal(rng, dims, jnp.float32)
    if shards:
        values = values * steps_of(rng, dims, shards, -0.22, 0.18)
    return jnp.clip(values, -bound, bound).astype(held_as)


def setup_inputs(seed: int = 0) -> dict:
    key_list = jax.random.split(jax.random.key(seed), 14)
    return {
        "queries": normal_values(key_list[0], (TOKEN_COUNT, HEADS * DK), 1.0, 6.0, ((0, 32), (1, 8))),
        "keys": normal_values(key_list[1], (TOKEN_COUNT, HEADS * DK), 1.0, 6.0, ((0, 32), (1, 8))),
        "values": normal_values(key_list[2], (TOKEN_COUNT, HEADS * DK), 1.0, 6.0, ((0, 32), (1, 8))),
        "out_gate": normal_values(key_list[3], (TOKEN_COUNT, HEADS * DK), 1.0, 6.0, ((0, 32), (1, 8))),
        "decay_log": draw_decay_log(jax.random.fold_in(key_list[13], 71), 0),
        "beta": draw_beta(jax.random.fold_in(key_list[13], 71), 0),
        "w_out": normal_values(key_list[6], (HEADS * DK, D), (HEADS * DK) ** -0.5, 0.125, ((0, 8),)),
        "resid": normal_values(key_list[7], (TOKEN_COUNT, D), 1.0, 6.0, ((0, 256),)),
        "norm_gain": jnp.clip(1.0 + 0.18 * jax.random.normal(key_list[8], (D,), jnp.float32), 0.1, 1.9),
        "router": normal_values(key_list[9], (D, EXPERTS), D ** -0.5, 0.1875),
        "w_gate_up": normal_values(key_list[10], (EXPERTS, D, 2 * FF), D ** -0.5, 0.1875, ((0, 256),)),
        "w_down": normal_values(key_list[11], (EXPERTS, FF, D), FF ** -0.5, 0.1875, ((0, 256),)),
        "block_experts": draw_block_experts(jax.random.fold_in(key_list[13], 71), 0),
    }


precise = lax.Precision.HIGHEST
route_scale = 2.446
epsilon = 1e-06

def unit_rows(array):
    return array * lax.rsqrt(lax.optimization_barrier(jnp.sum(array * array, axis=-1, keepdims=True)) + epsilon)

def reference(queries, keys, values, out_gate, decay_log, beta, w_out, resid, norm_gain, router, w_gate_up, w_down, block_experts):

    def per_head(array):
        return array.astype(jnp.float32).reshape(TOKEN_COUNT, HEADS, DK)
    query_unit = unit_rows(per_head(queries))
    key_unit = unit_rows(per_head(keys))
    value_heads = per_head(values)
    keep_rates = jnp.exp(per_head(decay_log))
    write_rates = beta.T

    def advance(state, inputs):
        query_row, key_row, value_row, keep_row, write_row = inputs
        faded = keep_row[:, :, None] * state
        guess = jnp.einsum('hd,hde->he', key_row, faded, precision=precise)
        state = faded + write_row[:, None, None] * key_row[:, :, None] * (value_row - guess)[:, None, :]
        return (state, jnp.einsum('hd,hde->he', query_row, state, precision=precise))
    start_state = jnp.zeros((HEADS, DK, DK), jnp.float32)
    _, head_out = lax.scan(advance, start_state, (query_unit, key_unit, value_heads, keep_rates, write_rates))
    scaled = head_out * lax.rsqrt(lax.optimization_barrier(jnp.mean(head_out * head_out, axis=-1, keepdims=True)) + epsilon)
    gated_heads = scaled * jax.nn.sigmoid(per_head(out_gate))
    mixed_heads = gated_heads.reshape(TOKEN_COUNT, HEADS * DK).astype(jnp.bfloat16)
    hidden_state = resid.astype(jnp.float32) + jnp.dot(mixed_heads, w_out, preferred_element_type=jnp.float32)
    normed = (hidden_state * lax.rsqrt(lax.optimization_barrier(jnp.mean(hidden_state * hidden_state, axis=-1, keepdims=True)) + epsilon) * norm_gain).astype(jnp.bfloat16)
    block_rows = normed.reshape(BLOCKS, TOK_DEV, D)

    def one_block(inputs):
        rows, expert_ids = inputs
        scores = jax.nn.sigmoid(jnp.dot(rows, jnp.take(router, expert_ids, axis=1), preferred_element_type=jnp.float32))
        gate_weights = route_scale * scores / lax.optimization_barrier(jnp.sum(scores, axis=1, keepdims=True))

        def one_expert(expert_id):
            gate_up = jnp.dot(rows, w_gate_up[expert_id], preferred_element_type=jnp.float32)
            expert_hidden = (jax.nn.silu(gate_up[:, :FF]) * gate_up[:, FF:]).astype(jnp.bfloat16)
            return jnp.dot(expert_hidden, w_down[expert_id], preferred_element_type=jnp.float32).astype(jnp.bfloat16)
        expert_out = lax.map(one_expert, expert_ids)
        return lax.optimization_barrier(jnp.sum(gate_weights.T[:, :, None] * expert_out.astype(jnp.float32), axis=0))
    combined = lax.map(one_block, (block_rows, block_experts)).reshape(TOKEN_COUNT, D)
    return (hidden_state + combined).astype(jnp.bfloat16)
```

```python
import functools

import jax
import jax.numpy as jnp
from jax import lax
from jax.experimental import pallas as pl
from jax.experimental.pallas import tpu as pltpu
from jax.sharding import PartitionSpec as P

DK = 128
TOPK = 8
CH = 64
PAIR = 128
STEP = 256
NEAR = 8
FAR = 4
F32, BF16 = jnp.float32, jnp.bfloat16
MESH = pl.DeviceIdType.MESH
NN = (((1,), (0,)), ((), ()))
NT = (((1,), (1,)), ((), ()))
TN = (((0,), (0,)), ((), ()))

route_scale = 2.446
epsilon = 1e-06


def split(a):
    high = a.astype(BF16)
    return high, (a - high.astype(F32)).astype(BF16)


def mm(a, b, dims=NN):
    return lax.dot_general(a, b, dims, preferred_element_type=F32)


def dot1(a, b, dims=NN):
    return mm(a.astype(BF16), b.astype(BF16), dims)


def dot3(a, b, dims=NN):
    ah, al = split(a)
    bh, bl = split(b)
    return mm(ah, bh, dims) + (mm(ah, bl, dims) + mm(al, bh, dims))


def unit(x):
    return x * lax.rsqrt(jnp.sum(x * x, axis=-1, keepdims=True) + epsilon)


def delta_kernel(q_ref, k_ref, v_ref, d_ref, b_ref, qo_ref, oo_ref, mb_ref, state):
    heads = q_ref.shape[1] // 128
    step = pl.program_id(0)
    row = lax.broadcasted_iota(jnp.int32, (PAIR, PAIR), 0)
    col = lax.broadcasted_iota(jnp.int32, (PAIR, PAIR), 1)

    @pl.when(step == 0)
    def _():
        eye = jnp.where(row == col, 1.0, 0.0).astype(F32)
        for h in range(heads):
            state[h, :, :128] = eye
            state[h, :, 128:] = jnp.zeros((128, 128), F32)

    same = (row // CH) == (col // CH)
    incl = same & (col <= row)
    strict = same & (col < row)
    tri = jnp.where(incl, 1.0, 0.0).astype(BF16)
    eye = jnp.where(row == col, 1.0, 0.0).astype(F32)
    work = {}
    for p in range(STEP // PAIR):
        rows = pl.ds(p * PAIR, PAIR)
        log = d_ref[rows, :]
        l1 = log.astype(BF16)
        r1 = log - l1.astype(F32)
        l2 = r1.astype(BF16)
        l3 = (r1 - l2.astype(F32)).astype(BF16)
        acc = mm(tri, l1) + (mm(tri, l2) + mm(tri, l3))
        top = lax.broadcasted_iota(jnp.int32, acc.shape, 0) < CH
        last = jnp.where(top, acc[CH - 1 : CH, :], acc[PAIR - 1 : PAIR, :])
        grow = jnp.exp(acc)
        shrink = jnp.exp(-acc)
        tail = jnp.exp(last - acc)
        total = jnp.exp(last)
        for h in range(heads):
            cols = pl.ds(h * 128, 128)
            hs = slice(h * 128, h * 128 + 128)
            key = unit(k_ref[rows, cols].astype(F32))
            query = unit(q_ref[rows, cols].astype(F32))
            beta = b_ref[rows, h : h + 1]
            key_hat = key * grow[:, hs]
            key_inv = key * shrink[:, hs]
            key_end = key * tail[:, hs]
            query_hat = query * grow[:, hs]
            low = jnp.where(strict, dot3(key_hat, key_inv, NT) * beta, 0.0)
            score = jnp.where(incl, dot1(query_hat, key_inv, NT), 0.0)
            inv = eye - jnp.where((row // 2 == col // 2), low, 0.0)
            size = 2
            while size < CH:
                part = jnp.where((row // (2 * size) == col // (2 * size)) & (row // size != col // size), low, 0.0)
                inv = inv - dot3(inv, dot3(part, inv))
                size *= 2
            right = jnp.concatenate([beta * key_hat, beta * v_ref[rows, cols].astype(F32)], axis=1)
            solved = dot3(inv, right)
            work[p, h] = (solved, score, query_hat, key_end, total[:, hs])
    zero = jnp.zeros((CH, 128), F32)
    for h in range(heads):
        cur = state[h]
        for p in range(STEP // PAIR):
            solved, score, query_hat, key_end, total = work[p, h]
            for half in range(2):
                rs = slice(half * CH, half * CH + CH)
                lead = dot3(jnp.concatenate([solved[rs, :128], query_hat[rs]], axis=0), cur)
                upd = jnp.concatenate([zero, solved[rs, 128:]], axis=1) - lead[:CH]
                out = lead[CH:] + dot1(score[rs, rs], upd)
                at = pl.ds(p * PAIR + half * CH, CH)
                qo_ref[at, h * 128 : h * 128 + 128] = out[:, :128].astype(qo_ref.dtype)
                oo_ref[at, h * 128 : h * 128 + 128] = out[:, 128:]
                fade = jnp.transpose(total[half * CH : half * CH + 8, :])[:, :1]
                cur = fade * cur + dot3(key_end[rs], upd, TN)
        state[h] = cur

    @pl.when(step == pl.num_programs(0) - 1)
    def _():
        for h in range(heads):
            mb_ref[h] = state[h].astype(mb_ref.dtype)


def delta(q, k, v, d, bt):
    rows, width = q.shape
    heads = width // 128
    spec = pl.BlockSpec((STEP, width), lambda i: (i, 0))
    return pl.pallas_call(
        delta_kernel,
        grid=(rows // STEP,),
        out_shape=(
            jax.ShapeDtypeStruct((rows, width), BF16),
            jax.ShapeDtypeStruct((rows, width), F32),
            jax.ShapeDtypeStruct((heads, 128, 256), BF16),
        ),
        in_specs=[spec, spec, spec, spec, pl.BlockSpec((STEP, heads), lambda i: (i, 0))],
        out_specs=(spec, spec, pl.BlockSpec((heads, 128, 256), lambda i: (0, 0, 0))),
        scratch_shapes=[pltpu.VMEM((heads, 128, 256), F32)],
        compiler_params=pltpu.CompilerParams(vmem_limit_bytes=40 * 2**20),
        cost_estimate=pl.CostEstimate(flops=5_000_000_000, bytes_accessed=6_000_000, transcendentals=0),
        name="delta_chunks",
    )(q, k, v, d, bt)


def mixer_kernel(
    mb_ref, q_ref, o_ref, gate_ref, resid_ref, gain_ref, w_ref, hidden_ref, normed_ref,
    near, far, total, mixed, mix, wide, near_s, near_r, far_s, far_r, mix_s, mix_r, w_sem,
):
    heads = mb_ref.shape[0]
    seq, exp = lax.axis_index("seq"), lax.axis_index("exp")
    group, slot = seq // NEAR, seq % NEAR
    exps = mix.shape[0]
    rows = normed_ref.shape[0]
    fetch = pltpu.make_async_copy(w_ref, wide, w_sem)
    fetch.start()
    barrier = pltpu.get_barrier_semaphore()
    for d in range(1, NEAR):
        peer = {"seq": group * NEAR + (slot + d) % NEAR}
        pl.semaphore_signal(barrier, inc=1, device_id=peer, device_id_type=MESH)
    for d in range(1, FAR):
        peer = {"seq": ((group + d) % FAR) * NEAR + slot}
        pl.semaphore_signal(barrier, inc=1, device_id=peer, device_id_type=MESH)
    for d in range(1, exps):
        pl.semaphore_signal(barrier, inc=1, device_id={"exp": (exp + d) % exps}, device_id_type=MESH)
    pl.semaphore_wait(barrier, NEAR + FAR + exps - 3)

    def near_copy(peer, place):
        return pltpu.make_async_remote_copy(
            src_ref=mb_ref, dst_ref=near.at[place], send_sem=near_s.at[peer], recv_sem=near_r.at[place],
            device_id={"seq": group * NEAR + peer}, device_id_type=MESH)

    def far_copy(peer, place):
        return pltpu.make_async_remote_copy(
            src_ref=total, dst_ref=far.at[place], send_sem=far_s.at[peer], recv_sem=far_r.at[place],
            device_id={"seq": peer * NEAR + slot}, device_id_type=MESH)

    def mix_copy(peer, place):
        return pltpu.make_async_remote_copy(
            src_ref=mixed.at[peer], dst_ref=mix.at[place], send_sem=mix_s.at[peer], recv_sem=mix_r.at[place],
            device_id={"exp": peer}, device_id_type=MESH)

    for d in range(1, NEAR):
        near_copy((slot + d) % NEAR, slot).start()
    near[slot] = mb_ref[...]
    row = lax.broadcasted_iota(jnp.int32, (128, 256), 0)
    col = lax.broadcasted_iota(jnp.int32, (128, 256), 1)
    start = jnp.where(row == col, 1.0, 0.0).astype(F32)
    shifts = col >= 128

    def apply(block, carried):
        high, low = split(carried)
        lead = block[:, :128]
        return mm(lead, high) + mm(lead, low)

    cur = [start] * heads
    before = [start] * heads
    for j in range(NEAR):
        @pl.when(j != slot)
        def _():
            near_copy(j, j).wait_recv()

        for h in range(heads):
            before[h] = jnp.where(slot == j, cur[h], before[h])
            block = near[j, h]
            cur[h] = apply(block, cur[h]) + jnp.where(shifts, block.astype(F32), 0.0)
    for h in range(heads):
        total[h] = cur[h].astype(BF16)
    for d in range(1, FAR):
        far_copy((group + d) % FAR, group).start()
    far[group] = total[...]
    state = [jnp.zeros((128, 128), F32)] * heads
    for g in range(FAR):
        @pl.when(g != group)
        def _():
            far_copy(g, g).wait_recv()

        for h in range(heads):
            block = far[g, h]
            moved = apply(block, state[h]) + block[:, 128:].astype(F32)
            state[h] = jnp.where(g < group, moved, state[h])
    parts = []
    for h in range(heads):
        entering = dot3(before[h][:, :128], state[h]) + before[h][:, 128:]
        parts.append(split(entering))

    def mix_rows(peer):
        at = pl.ds(pl.multiple_of(peer * rows, rows), rows)
        for h in range(heads):
            cols = pl.ds(h * 128, 128)
            query = q_ref[at, cols]
            out = mm(query, parts[h][0]) + mm(query, parts[h][1]) + o_ref[at, cols]
            out = out * lax.rsqrt(jnp.mean(out * out, axis=-1, keepdims=True) + epsilon)
            gate = gate_ref[at, cols].astype(F32)
            mixed[peer, :, cols] = (out / (1.0 + jnp.exp(-gate))).astype(BF16)

    for d in range(1, exps):
        peer = (exp + d) % exps
        mix_rows(peer)
        mix_copy(peer, exp).start()
    mix_rows(exp)
    mix[exp] = mixed[exp]
    fetch.wait()
    acc = resid_ref[...].astype(F32)
    for d in range(exps):
        source = (exp + exps - d) % exps
        if d:
            mix_copy(source, source).wait_recv()
        wrows = pl.ds(pl.multiple_of(source * 256, 256), 256)
        acc = acc + mm(mix[source], wide[wrows, :])
    hidden_ref[...] = acc
    scale = lax.rsqrt(jnp.mean(acc * acc, axis=-1, keepdims=True) + epsilon)
    normed_ref[...] = (acc * scale * gain_ref[...]).astype(BF16)
    for d in range(1, NEAR):
        near_copy((slot + d) % NEAR, slot).wait_send()
    for d in range(1, FAR):
        far_copy((group + d) % FAR, group).wait_send()
    for d in range(1, exps):
        mix_copy((exp + d) % exps, exp).wait_send()


def mixer(mb, q, o, gate, resid, gain, w_full, exps):
    rows, width = resid.shape
    heads = mb.shape[0]
    vmem = pl.BlockSpec(memory_space=pltpu.VMEM)
    dma = pltpu.SemaphoreType.DMA
    return pl.pallas_call(
        mixer_kernel,
        out_shape=(
            jax.ShapeDtypeStruct((rows, width), F32),
            jax.ShapeDtypeStruct((rows, width), BF16),
        ),
        in_specs=[vmem] * 6 + [pl.BlockSpec(memory_space=pl.ANY)],
        out_specs=(vmem, vmem),
        scratch_shapes=[
            pltpu.VMEM((NEAR, heads, 128, 256), BF16),
            pltpu.VMEM((FAR, heads, 128, 256), BF16),
            pltpu.VMEM((heads, 128, 256), BF16),
            pltpu.VMEM((exps, rows, heads * 128), BF16),
            pltpu.VMEM((exps, rows, heads * 128), BF16),
            pltpu.VMEM(w_full.shape, BF16),
            dma((NEAR,)), dma((NEAR,)), dma((FAR,)), dma((FAR,)), dma((exps,)), dma((exps,)), dma,
        ],
        compiler_params=pltpu.CompilerParams(
            collective_id=0, has_side_effects=True, vmem_limit_bytes=48 * 2**20
        ),
        name="mixer",
    )(mb, q, o, gate, resid, gain, w_full)


def local(
    queries,
    keys,
    values,
    out_gate,
    decay_log,
    beta,
    w_out,
    resid,
    norm_gain,
    router,
    w_gate_up,
    w_down,
    block_experts,
):
    seq_count = lax.axis_size("seq")
    exp_count = lax.axis_size("exp")
    tok_rows, model_width = resid.shape
    w_full = lax.all_gather(w_out, "exp", axis=0, tiled=True)
    q_lead, o_lead, carried = delta(queries, keys, values, decay_log, beta.T)
    hidden_state, normed = mixer(
        carried, q_lead, o_lead, out_gate, resid, norm_gain.reshape(1, -1), w_full, exp_count
    )
    seq_index = lax.axis_index("seq")
    exp_index = lax.axis_index("exp")
    per_column = TOPK // exp_count
    capacity = 2 * min(TOPK - 1, seq_count // 2)
    layout = block_experts.reshape(seq_count, exp_count, per_column, exp_count)
    column_pick = jnp.arange(exp_count) == exp_index
    row_blocks = lax.all_gather(normed, "exp", axis=0, tiled=True).reshape(
        exp_count, tok_rows, model_width
    )
    own_table = lax.dynamic_index_in_dim(layout, seq_index, 0, keepdims=False)
    sent_experts = jnp.sum(jnp.where(column_pick, own_table, 0), axis=2).reshape(TOPK)
    dest_rows = sent_experts // exp_count
    row_match = dest_rows[None, :] == jnp.arange(seq_count)[:, None]
    copy_block = jnp.arange(TOPK) // per_column
    source_block = jnp.sum(jnp.where(row_match, copy_block[None, :], 0), axis=1)
    outgoing = jnp.take(row_blocks, source_block, axis=0)
    my_expert = seq_index * exp_count + exp_index
    column_experts = jnp.sum(jnp.where(column_pick, layout, 0), axis=3)
    present = jnp.any(column_experts == my_expert, axis=(1, 2))
    slot_rank = jnp.cumsum(present.astype(jnp.int32)) - 1
    slot_hit = present[None, :] & (slot_rank[None, :] == jnp.arange(capacity)[:, None])
    pick_rows = jnp.sum(jnp.where(slot_hit, jnp.arange(seq_count)[None, :], 0), axis=1)
    hidden_width = w_down.shape[1]
    incoming_blocks = lax.all_to_all(outgoing, "seq", split_axis=0, concat_axis=0, tiled=True)
    packed_blocks = jnp.take(incoming_blocks, pick_rows, axis=0)
    rows_here = packed_blocks.shape[1]
    packed = packed_blocks.reshape(capacity * rows_here, model_width)
    gate_up = jnp.dot(packed, w_gate_up[0], preferred_element_type=jnp.float32)
    expert_hidden = (jax.nn.silu(gate_up[:, :hidden_width]) * gate_up[:, hidden_width:]).astype(
        jnp.bfloat16
    )
    expert_out = jnp.dot(expert_hidden, w_down[0], preferred_element_type=jnp.float32).astype(
        jnp.bfloat16
    )
    expert_out = expert_out.reshape(capacity, rows_here, model_width)
    returned = lax.all_to_all(
        jnp.take(expert_out, jnp.maximum(slot_rank, 0), axis=0),
        "seq",
        split_axis=0,
        concat_axis=0,
        tiled=True,
    )
    per_copy = jnp.take(returned, dest_rows, axis=0).reshape(
        exp_count, per_column, tok_rows, model_width
    )
    collected = lax.all_to_all(per_copy, "exp", split_axis=0, concat_axis=0, tiled=True).reshape(
        TOPK, tok_rows, model_width
    )
    my_ids = lax.dynamic_index_in_dim(block_experts, my_expert, 0, keepdims=False)
    ordered_ids = my_ids.reshape(per_column, exp_count).T.reshape(TOPK)
    router_cols = jnp.take(router, ordered_ids, axis=1)
    scores = jax.nn.sigmoid(jnp.dot(normed, router_cols, preferred_element_type=jnp.float32))
    gate_weights = route_scale * scores / jnp.sum(scores, axis=1, keepdims=True)
    combined = jnp.sum(gate_weights.T[:, :, None] * collected.astype(jnp.float32), axis=0)
    return (hidden_state + combined).astype(jnp.bfloat16)


def solution(mesh):
    return jax.shard_map(
        local,
        mesh=mesh,
        in_specs=(
            P("seq", "exp"),
            P("seq", "exp"),
            P("seq", "exp"),
            P("seq", "exp"),
            P("seq", "exp"),
            P("exp", "seq"),
            P("exp", None),
            P(("seq", "exp"), None),
            P(),
            P(),
            P(("seq", "exp"), None, None),
            P(("seq", "exp"), None, None),
            P(),
        ),
        out_specs=P(("seq", "exp"), None),
        check_vma=False,
    )
```

```python
import functools

import jax
import jax.numpy as jnp
from jax import lax
from jax.experimental import pallas as pl
from jax.experimental.pallas import tpu as pltpu
from jax.sharding import PartitionSpec as P

DK = 128
TOPK = 8
CH = 64
PAIR = 128
STEP = 256
NEAR = 8
FAR = 4
F32, BF16 = jnp.float32, jnp.bfloat16
MESH = pl.DeviceIdType.MESH
NN = (((1,), (0,)), ((), ()))
NT = (((1,), (1,)), ((), ()))
TN = (((0,), (0,)), ((), ()))

route_scale = 2.446
epsilon = 1e-06


def split(a):
    high = a.astype(BF16)
    return high, (a - high.astype(F32)).astype(BF16)


def mm(a, b, dims=NN):
    return lax.dot_general(a, b, dims, preferred_element_type=F32)


def dot1(a, b, dims=NN):
    return mm(a.astype(BF16), b.astype(BF16), dims)


def dot3(a, b, dims=NN):
    ah, al = split(a)
    bh, bl = split(b)
    return mm(ah, bh, dims) + (mm(ah, bl, dims) + mm(al, bh, dims))


def unit(x):
    return x * lax.rsqrt(jnp.sum(x * x, axis=-1, keepdims=True) + epsilon)


def delta_kernel(q_ref, k_ref, v_ref, d_ref, b_ref, qo_ref, oo_ref, mb_ref, state):
    heads = q_ref.shape[1] // 128
    step = pl.program_id(0)
    row = lax.broadcasted_iota(jnp.int32, (PAIR, PAIR), 0)
    col = lax.broadcasted_iota(jnp.int32, (PAIR, PAIR), 1)

    @pl.when(step == 0)
    def _():
        eye = jnp.where(row == col, 1.0, 0.0).astype(F32)
        for h in range(heads):
            state[h, :, :128] = eye
            state[h, :, 128:] = jnp.zeros((128, 128), F32)

    same = (row // CH) == (col // CH)
    incl = same & (col <= row)
    strict = same & (col < row)
    tri = jnp.where(incl, 1.0, 0.0).astype(BF16)
    eye = jnp.where(row == col, 1.0, 0.0).astype(F32)
    work = {}
    for p in range(STEP // PAIR):
        rows = pl.ds(p * PAIR, PAIR)
        log = d_ref[rows, :]
        l1 = log.astype(BF16)
        r1 = log - l1.astype(F32)
        l2 = r1.astype(BF16)
        l3 = (r1 - l2.astype(F32)).astype(BF16)
        acc = mm(tri, l1) + (mm(tri, l2) + mm(tri, l3))
        top = lax.broadcasted_iota(jnp.int32, acc.shape, 0) < CH
        last = jnp.where(top, acc[CH - 1 : CH, :], acc[PAIR - 1 : PAIR, :])
        grow = jnp.exp(acc)
        shrink = jnp.exp(-acc)
        tail = jnp.exp(last - acc)
        total = jnp.exp(last)
        for h in range(heads):
            cols = pl.ds(h * 128, 128)
            hs = slice(h * 128, h * 128 + 128)
            key = unit(k_ref[rows, cols].astype(F32))
            query = unit(q_ref[rows, cols].astype(F32))
            beta = b_ref[rows, h : h + 1]
            key_hat = key * grow[:, hs]
            key_inv = key * shrink[:, hs]
            key_end = key * tail[:, hs]
            query_hat = query * grow[:, hs]
            low = jnp.where(strict, dot3(key_hat, key_inv, NT) * beta, 0.0)
            score = jnp.where(incl, dot1(query_hat, key_inv, NT), 0.0)
            inv = eye - jnp.where((row // 2 == col // 2), low, 0.0)
            size = 2
            while size < CH:
                part = jnp.where((row // (2 * size) == col // (2 * size)) & (row // size != col // size), low, 0.0)
                inv = inv - dot3(inv, dot3(part, inv))
                size *= 2
            right = jnp.concatenate([beta * key_hat, beta * v_ref[rows, cols].astype(F32)], axis=1)
            solved = dot3(inv, right)
            work[p, h] = (solved, score, query_hat, key_end, total[:, hs])
    zero = jnp.zeros((CH, 128), F32)
    for h in range(heads):
        cur = state[h]
        for p in range(STEP // PAIR):
            solved, score, query_hat, key_end, total = work[p, h]
            for half in range(2):
                rs = slice(half * CH, half * CH + CH)
                lead = dot3(jnp.concatenate([solved[rs, :128], query_hat[rs]], axis=0), cur)
                upd = jnp.concatenate([zero, solved[rs, 128:]], axis=1) - lead[:CH]
                out = lead[CH:] + dot1(score[rs, rs], upd)
                at = pl.ds(p * PAIR + half * CH, CH)
                qo_ref[at, h * 128 : h * 128 + 128] = out[:, :128].astype(qo_ref.dtype)
                oo_ref[at, h * 128 : h * 128 + 128] = out[:, 128:]
                fade = jnp.transpose(total[half * CH : half * CH + 8, :])[:, :1]
                cur = fade * cur + dot3(key_end[rs], upd, TN)
        state[h] = cur

    @pl.when(step == pl.num_programs(0) - 1)
    def _():
        for h in range(heads):
            mb_ref[h] = state[h].astype(mb_ref.dtype)


def delta(q, k, v, d, bt):
    rows, width = q.shape
    heads = width // 128
    spec = pl.BlockSpec((STEP, width), lambda i: (i, 0))
    return pl.pallas_call(
        delta_kernel,
        grid=(rows // STEP,),
        out_shape=(
            jax.ShapeDtypeStruct((rows, width), BF16),
            jax.ShapeDtypeStruct((rows, width), F32),
            jax.ShapeDtypeStruct((heads, 128, 256), BF16),
        ),
        in_specs=[spec, spec, spec, spec, pl.BlockSpec((STEP, heads), lambda i: (i, 0))],
        out_specs=(spec, spec, pl.BlockSpec((heads, 128, 256), lambda i: (0, 0, 0))),
        scratch_shapes=[pltpu.VMEM((heads, 128, 256), F32)],
        compiler_params=pltpu.CompilerParams(vmem_limit_bytes=40 * 2**20),
        cost_estimate=pl.CostEstimate(flops=5_000_000_000, bytes_accessed=6_000_000, transcendentals=0),
        name="delta_chunks",
    )(q, k, v, d, bt)


def mixer_kernel(
    mb_ref, q_ref, o_ref, gate_ref, resid_ref, gain_ref, w_ref, hidden_ref, normed_ref,
    near, far, total, mixed, mix, wide, near_s, near_r, far_s, far_r, mix_s, mix_r, w_sem,
):
    heads = mb_ref.shape[0]
    seq, exp = lax.axis_index("seq"), lax.axis_index("exp")
    group, slot = seq // NEAR, seq % NEAR
    exps = mix.shape[0]
    rows = normed_ref.shape[0]
    fetch = pltpu.make_async_copy(w_ref, wide, w_sem)
    fetch.start()
    barrier = pltpu.get_barrier_semaphore()
    for d in range(1, NEAR):
        peer = {"seq": group * NEAR + (slot + d) % NEAR}
        pl.semaphore_signal(barrier, inc=1, device_id=peer, device_id_type=MESH)
    for d in range(1, FAR):
        peer = {"seq": ((group + d) % FAR) * NEAR + slot}
        pl.semaphore_signal(barrier, inc=1, device_id=peer, device_id_type=MESH)
    for d in range(1, exps):
        pl.semaphore_signal(barrier, inc=1, device_id={"exp": (exp + d) % exps}, device_id_type=MESH)
    pl.semaphore_wait(barrier, NEAR + FAR + exps - 3)

    def near_copy(peer, place):
        return pltpu.make_async_remote_copy(
            src_ref=mb_ref, dst_ref=near.at[place], send_sem=near_s.at[peer], recv_sem=near_r.at[place],
            device_id={"seq": group * NEAR + peer}, device_id_type=MESH)

    def far_copy(peer, place):
        return pltpu.make_async_remote_copy(
            src_ref=total, dst_ref=far.at[place], send_sem=far_s.at[peer], recv_sem=far_r.at[place],
            device_id={"seq": peer * NEAR + slot}, device_id_type=MESH)

    def mix_copy(peer, place):
        return pltpu.make_async_remote_copy(
            src_ref=mixed.at[peer], dst_ref=mix.at[place], send_sem=mix_s.at[peer], recv_sem=mix_r.at[place],
            device_id={"exp": peer}, device_id_type=MESH)

    for d in range(1, NEAR):
        near_copy((slot + d) % NEAR, slot).start()
    near[slot] = mb_ref[...]
    row = lax.broadcasted_iota(jnp.int32, (128, 256), 0)
    col = lax.broadcasted_iota(jnp.int32, (128, 256), 1)
    start = jnp.where(row == col, 1.0, 0.0).astype(F32)
    shifts = col >= 128

    def apply(block, carried):
        high, low = split(carried)
        lead = block[:, :128]
        return mm(lead, high) + mm(lead, low)

    cur = [start] * heads
    before = [start] * heads
    for j in range(NEAR):
        @pl.when(j != slot)
        def _():
            near_copy(j, j).wait_recv()

        for h in range(heads):
            before[h] = jnp.where(slot == j, cur[h], before[h])
            block = near[j, h]
            cur[h] = apply(block, cur[h]) + jnp.where(shifts, block.astype(F32), 0.0)
    for h in range(heads):
        total[h] = cur[h].astype(BF16)
    for d in range(1, FAR):
        far_copy((group + d) % FAR, group).start()
    far[group] = total[...]
    state = [jnp.zeros((128, 128), F32)] * heads
    for g in range(FAR):
        @pl.when(g != group)
        def _():
            far_copy(g, g).wait_recv()

        for h in range(heads):
            block = far[g, h]
            moved = apply(block, state[h]) + block[:, 128:].astype(F32)
            state[h] = jnp.where(g < group, moved, state[h])
    parts = []
    for h in range(heads):
        entering = dot3(before[h][:, :128], state[h]) + before[h][:, 128:]
        parts.append(split(entering))

    def mix_rows(peer):
        at = pl.ds(pl.multiple_of(peer * rows, rows), rows)
        for h in range(heads):
            cols = pl.ds(h * 128, 128)
            query = q_ref[at, cols]
            out = mm(query, parts[h][0]) + mm(query, parts[h][1]) + o_ref[at, cols]
            out = out * lax.rsqrt(jnp.mean(out * out, axis=-1, keepdims=True) + epsilon)
            gate = gate_ref[at, cols].astype(F32)
            mixed[peer, :, cols] = (out / (1.0 + jnp.exp(-gate))).astype(BF16)

    for d in range(1, exps):
        peer = (exp + d) % exps
        mix_rows(peer)
        mix_copy(peer, exp).start()
    mix_rows(exp)
    mix[exp] = mixed[exp]
    fetch.wait()
    acc = resid_ref[...].astype(F32)
    for d in range(exps):
        source = (exp + exps - d) % exps
        if d:
            mix_copy(source, source).wait_recv()
        wrows = pl.ds(pl.multiple_of(source * 256, 256), 256)
        acc = acc + mm(mix[source], wide[wrows, :])
    hidden_ref[...] = acc
    scale = lax.rsqrt(jnp.mean(acc * acc, axis=-1, keepdims=True) + epsilon)
    normed_ref[...] = (acc * scale * gain_ref[...]).astype(BF16)
    for d in range(1, NEAR):
        near_copy((slot + d) % NEAR, slot).wait_send()
    for d in range(1, FAR):
        far_copy((group + d) % FAR, group).wait_send()
    for d in range(1, exps):
        mix_copy((exp + d) % exps, exp).wait_send()


def mixer(mb, q, o, gate, resid, gain, w_full, exps):
    rows, width = resid.shape
    heads = mb.shape[0]
    vmem = pl.BlockSpec(memory_space=pltpu.VMEM)
    dma = pltpu.SemaphoreType.DMA
    return pl.pallas_call(
        mixer_kernel,
        out_shape=(
            jax.ShapeDtypeStruct((rows, width), F32),
            jax.ShapeDtypeStruct((rows, width), BF16),
        ),
        in_specs=[vmem] * 6 + [pl.BlockSpec(memory_space=pl.ANY)],
        out_specs=(vmem, vmem),
        scratch_shapes=[
            pltpu.VMEM((NEAR, heads, 128, 256), BF16),
            pltpu.VMEM((FAR, heads, 128, 256), BF16),
            pltpu.VMEM((heads, 128, 256), BF16),
            pltpu.VMEM((exps, rows, heads * 128), BF16),
            pltpu.VMEM((exps, rows, heads * 128), BF16),
            pltpu.VMEM(w_full.shape, BF16),
            dma((NEAR,)), dma((NEAR,)), dma((FAR,)), dma((FAR,)), dma((exps,)), dma((exps,)), dma,
        ],
        compiler_params=pltpu.CompilerParams(
            collective_id=0, has_side_effects=True, vmem_limit_bytes=48 * 2**20
        ),
        name="mixer",
    )(mb, q, o, gate, resid, gain, w_full)


def expert_kernel(
    normed_ref, hidden_ref, table_ref, router_ref, wgu_ref, wd_ref, out_ref,
    spread, landed, final, own, every, leave, arrive, inner, back, home, give, take, wgu, wd,
    fetch_s, spread_s, spread_r, every_s, every_r, leave_s, leave_r, back_s, back_r, give_s, give_r, end_s, end_r,
):
    seq, exp = lax.axis_index("seq"), lax.axis_index("exp")
    seqs, exps = lax.axis_size("seq"), lax.axis_size("exp")
    width = normed_ref.shape[1]
    third = width // 3
    parts = every.shape[0]
    group = every.shape[2]
    hidden_width = wd.shape[0]
    core, across, along = seq % 2, (seq // 2) % 4, seq // 8
    load_up = pltpu.make_async_copy(wgu_ref, wgu, fetch_s.at[0])
    load_down = pltpu.make_async_copy(wd_ref, wd, fetch_s.at[1])
    load_up.start()
    load_down.start()

    def plane(p):
        step = p // 2
        turn = 1 + 2 * core
        dx = (step % 4) * turn
        dy = ((step // 4 + step) % 4) * turn
        return ((along + dy) % 4) * 8 + ((across + dx) % 4) * 2 + (core + p) % 2

    def column(d):
        return (exp + d) % exps

    barrier = pltpu.get_barrier_semaphore()

    @pl.loop(1, seqs)
    def _(p):
        pl.semaphore_signal(barrier, inc=1, device_id={"seq": plane(p)}, device_id_type=MESH)

    @pl.loop(1, exps)
    def _(d):
        pl.semaphore_signal(barrier, inc=1, device_id={"exp": column(d)}, device_id_type=MESH)

    row = lax.broadcasted_iota(jnp.int32, (512, 128), 0)
    col = lax.broadcasted_iota(jnp.int32, (512, 128), 1)
    place = (row % 16) // 4 * 32 + row // 16 == col
    to_wire = [jnp.where(place & (row % 4 == g), 1.0, 0.0).astype(BF16) for g in range(3)]
    row = lax.broadcasted_iota(jnp.int32, (128, 512), 0)
    col = lax.broadcasted_iota(jnp.int32, (128, 512), 1)
    place = (col % 16) // 4 * 32 + col // 16 == row
    from_wire = [jnp.where(place & (col % 4 == g), 1.0, 0.0).astype(BF16) for g in range(3)]

    def lay_out(rows):
        total = mm(to_wire[0], rows[:, :third])
        total = total + mm(to_wire[1], rows[:, third : 2 * third])
        total = total + mm(to_wire[2], rows[:, 2 * third :])
        spread[...] = total.astype(BF16)

    def wire(peer, place, target, send, recv):
        return pltpu.make_async_remote_copy(
            src_ref=spread.at[pl.ds(pl.multiple_of(peer * 16, 16), 16)],
            dst_ref=target.at[pl.ds(pl.multiple_of(place * 16, 16), 16)],
            send_sem=send, recv_sem=recv, device_id={"seq": peer}, device_id_type=MESH)

    def slots(source, target, part, peer, place, send, recv):
        return pltpu.make_async_remote_copy(
            src_ref=source.at[part, pl.ds(pl.multiple_of(peer * 16, 16), 16)],
            dst_ref=target.at[part, pl.ds(pl.multiple_of(place * 16, 16), 16)],
            send_sem=send.at[part], recv_sem=recv.at[part], device_id={"seq": peer}, device_id_type=MESH)

    def settle(view, sem):
        pltpu.make_async_copy(view, view, sem).wait()

    others = (seqs - 1) * 16
    mine = pl.ds(pl.multiple_of(seq * 16, 16), 16)

    lay_out(normed_ref[...])
    pl.semaphore_wait(barrier, seqs + exps - 2)

    @pl.loop(1, seqs)
    def _(p):
        wire(plane(p), seq, landed, spread_s, spread_r).start()

    landed[mine] = spread[mine]

    table = table_ref[...]
    lane = lax.broadcasted_iota(jnp.int32, table.shape, 1)
    sub = lax.broadcasted_iota(jnp.int32, table.shape, 0)
    target = jnp.sum(jnp.where(sub == exp, table, 0), axis=0, keepdims=True) // exps
    hits = lax.broadcasted_iota(jnp.int32, (seqs, 256), 0) == target
    before = lax.broadcasted_iota(jnp.int32, (256, 256), 0) < lax.broadcasted_iota(jnp.int32, (256, 256), 1)
    counts = mm(jnp.where(hits, 1.0, 0.0).astype(BF16), jnp.where(before, 1.0, 0.0).astype(BF16))
    rank = jnp.sum(jnp.where(hits, counts, 0.0), axis=0, keepdims=True)
    goal = target.astype(F32) * 16.0 + rank
    pick = jnp.where(lax.broadcasted_iota(jnp.int32, (512, 256), 0).astype(F32) == goal, 1.0, 0.0)
    unpick = jnp.transpose(pick).astype(BF16)
    pick = pick.astype(BF16)
    ids = jnp.sum(jnp.where(lane == exp * seqs + seq, table, 0), axis=1, keepdims=True)
    chosen = jnp.sum(jnp.where(lane == ids, 1.0, 0.0), axis=0, keepdims=True)
    scores = mm(normed_ref[...], router_ref[...])
    denom = jnp.sum(chosen / (1.0 + jnp.exp(-scores)), axis=1, keepdims=True)
    here = lax.broadcasted_iota(jnp.int32, (256, 128), 0) == seq * exps + exp
    router_col = mm(router_ref[...], jnp.where(here, 1.0, 0.0).astype(BF16)).astype(BF16)

    settle(landed.at[pl.ds(0, others)], spread_r)
    settle(spread.at[pl.ds(0, others)], spread_s)
    for g in range(3):
        own[:, g * third : (g + 1) * third] = mm(from_wire[g], landed[...]).astype(BF16)

    def gather(part, peer, place):
        return pltpu.make_async_remote_copy(
            src_ref=own.at[pl.ds(pl.multiple_of(part * group, group), group)],
            dst_ref=every.at[part, place],
            send_sem=every_s.at[part], recv_sem=every_r.at[part], device_id={"exp": peer}, device_id_type=MESH)

    @pl.loop(0, parts)
    def _(part):
        @pl.loop(1, exps)
        def _(d):
            gather(part, column(d), exp).start()

        every[part, exp] = own[pl.ds(pl.multiple_of(part * group, group), group)]

    @pl.loop(0, parts)
    def _(part):
        settle(every.at[part, pl.ds(0, exps - 1)], every_r.at[part])
        rows = every[part].reshape(exps * group, width)
        leave[part] = mm(pick, rows).astype(BF16)

        @pl.loop(1, seqs)
        def _(p):
            slots(leave, arrive, part, plane(p), seq, leave_s, leave_r).start()

        arrive[part, mine] = leave[part, mine]

    load_up.wait()
    load_down.wait()

    @pl.loop(0, parts)
    def _(part):
        settle(arrive.at[part, pl.ds(0, others)], leave_r.at[part])
        score = 1.0 / (1.0 + jnp.exp(-mm(arrive[part], router_col)))

        @pl.loop(0, hidden_width // 256)
        def _(j):
            rows = arrive[part]
            left = mm(rows, wgu[:, pl.ds(pl.multiple_of(j * 256, 256), 256)])
            right = mm(rows, wgu[:, pl.ds(pl.multiple_of(hidden_width + j * 256, 256), 256)])
            inner[:, pl.ds(pl.multiple_of(j * 256, 256), 256)] = (left / (1.0 + jnp.exp(-left)) * right).astype(BF16)

        weight = jnp.concatenate([score] * 3, axis=1)
        for g in range(3):
            cols = pl.ds(g * third, third)
            back[part, :, cols] = (weight * mm(inner[...], wd[:, cols])).astype(BF16)

        @pl.loop(1, seqs)
        def _(p):
            slots(back, home, part, plane(p), seq, back_s, back_r).start()

        home[part, mine] = back[part, mine]

    def deliver(part, peer, place):
        return pltpu.make_async_remote_copy(
            src_ref=give.at[part, peer], dst_ref=take.at[part, place],
            send_sem=give_s.at[part], recv_sem=give_r.at[part], device_id={"exp": peer}, device_id_type=MESH)

    @pl.loop(0, parts)
    def _(part):
        settle(home.at[part, pl.ds(0, others)], back_r.at[part])
        give[part] = mm(unpick, home[part]).astype(BF16).reshape(exps, group, width)

        @pl.loop(1, exps)
        def _(d):
            deliver(part, column(d), exp).start()

        take[part, exp] = give[part, exp]

    @pl.loop(0, parts)
    def _(part):
        settle(take.at[part, pl.ds(0, exps - 1)], give_r.at[part])
        own_rows = pl.ds(pl.multiple_of(part * group, group), group)
        settle(every.at[part, pl.ds(0, exps - 1)], every_s.at[part])
        total = take[part, 0].astype(F32)
        for c in range(1, exps):
            total = total + take[part, c].astype(F32)
        own[own_rows] = total.astype(BF16)

    lay_out(own[...])

    @pl.loop(1, seqs)
    def _(p):
        wire(plane(p), seq, final, end_s, end_r).start()

    final[mine] = spread[mine]
    settle(final.at[pl.ds(0, others)], end_r)
    scale = route_scale / denom
    for g in range(3):
        cols = pl.ds(g * third, third)
        out_ref[:, cols] = (hidden_ref[:, cols] + scale * mm(from_wire[g], final[...])).astype(BF16)
    settle(spread.at[pl.ds(0, others)], end_s)

    @pl.loop(0, parts)
    def _(part):
        settle(leave.at[part, pl.ds(0, others)], leave_s.at[part])
        settle(back.at[part, pl.ds(0, others)], back_s.at[part])
        settle(give.at[part, pl.ds(0, exps - 1)], give_s.at[part])


def experts(normed, hidden, table, router, wgu, wd, seqs, exps):
    rows, width = normed.shape
    parts, group = rows // seqs, seqs
    held = seqs * 16
    vmem = pl.BlockSpec(memory_space=pltpu.VMEM)
    hbm = pl.BlockSpec(memory_space=pl.ANY)
    dma = pltpu.SemaphoreType.DMA
    slots = pltpu.VMEM((parts, held, width), BF16)
    blocks = pltpu.VMEM((parts, exps, group, width), BF16)
    small = pltpu.VMEM((held, width // 3), BF16)
    return pl.pallas_call(
        expert_kernel,
        out_shape=jax.ShapeDtypeStruct((rows, width), BF16),
        in_specs=[vmem] * 4 + [hbm] * 2,
        out_specs=vmem,
        scratch_shapes=[
            small, small, small, pltpu.VMEM((rows, width), BF16),
            blocks, slots, slots, pltpu.VMEM((held, wd.shape[0]), BF16), slots, slots, blocks, blocks,
            pltpu.VMEM(wgu.shape, BF16), pltpu.VMEM(wd.shape, BF16),
            dma((2,)), dma, dma, dma((parts,)), dma((parts,)), dma((parts,)), dma((parts,)),
            dma((parts,)), dma((parts,)), dma((parts,)), dma((parts,)), dma, dma,
        ],
        compiler_params=pltpu.CompilerParams(
            collective_id=1, has_side_effects=True, vmem_limit_bytes=56 * 2**20
        ),
        name="experts",
    )(normed, hidden, table, router, wgu, wd)


def local(
    queries,
    keys,
    values,
    out_gate,
    decay_log,
    beta,
    w_out,
    resid,
    norm_gain,
    router,
    w_gate_up,
    w_down,
    block_experts,
):
    seq_count = lax.axis_size("seq")
    exp_count = lax.axis_size("exp")
    tok_rows, model_width = resid.shape
    w_full = lax.all_gather(w_out, "exp", axis=0, tiled=True)
    q_lead, o_lead, carried = delta(queries, keys, values, decay_log, beta.T)
    hidden_state, normed = mixer(
        carried, q_lead, o_lead, out_gate, resid, norm_gain.reshape(1, -1), w_full, exp_count
    )
    table = block_experts.reshape(seq_count, exp_count, TOPK).transpose(2, 1, 0).reshape(TOPK, -1)
    return experts(normed, hidden_state, table, router, w_gate_up[0], w_down[0], seq_count, exp_count)


def solution(mesh):
    return jax.shard_map(
        local,
        mesh=mesh,
        in_specs=(
            P("seq", "exp"),
            P("seq", "exp"),
            P("seq", "exp"),
            P("seq", "exp"),
            P("seq", "exp"),
            P("exp", "seq"),
            P("exp", None),
            P(("seq", "exp"), None),
            P(),
            P(),
            P(("seq", "exp"), None, None),
            P(("seq", "exp"), None, None),
            P(),
        ),
        out_specs=P(("seq", "exp"), None),
        check_vma=False,
    )
```

```python
import functools

import jax
import jax.numpy as jnp
from jax import lax
from jax.experimental import pallas as pl
from jax.experimental.pallas import tpu as pltpu
from jax.sharding import PartitionSpec as P

DK = 128
TOPK = 8
CH = 64
PAIR = 128
STEP = 512
NEAR = 8
FAR = 4
F32, BF16 = jnp.float32, jnp.bfloat16
MESH = pl.DeviceIdType.MESH
NN = (((1,), (0,)), ((), ()))
NT = (((1,), (1,)), ((), ()))
TN = (((0,), (0,)), ((), ()))

route_scale = 2.446
epsilon = 1e-06


def split(a):
    high = a.astype(BF16)
    return high, (a - high.astype(F32)).astype(BF16)


def mm(a, b, dims=NN):
    return lax.dot_general(a, b, dims, preferred_element_type=F32)


def dot1(a, b, dims=NN):
    return mm(a.astype(BF16), b.astype(BF16), dims)


def dot3(a, b, dims=NN):
    ah, al = split(a)
    bh, bl = split(b)
    return mm(ah, bh, dims) + (mm(ah, bl, dims) + mm(al, bh, dims))


def unit(x):
    return x * lax.rsqrt(jnp.sum(x * x, axis=-1, keepdims=True) + epsilon)


def delta_kernel(q_ref, k_ref, v_ref, d_ref, b_ref, qo_ref, oo_ref, mb_ref, state):
    heads = q_ref.shape[1] // 128
    step = pl.program_id(0)
    row = lax.broadcasted_iota(jnp.int32, (PAIR, PAIR), 0)
    col = lax.broadcasted_iota(jnp.int32, (PAIR, PAIR), 1)

    @pl.when(step == 0)
    def _():
        eye = jnp.where(row == col, 1.0, 0.0).astype(F32)
        for h in range(heads):
            state[h, :, :128] = eye
            state[h, :, 128:] = jnp.zeros((128, 128), F32)

    same = (row // CH) == (col // CH)
    incl = same & (col <= row)
    strict = same & (col < row)
    tri = jnp.where(incl, 1.0, 0.0).astype(BF16)
    eye = jnp.where(row == col, 1.0, 0.0).astype(F32)
    first = (row // 2) == (col // 2)
    masks = []
    size = 2
    while size < CH:
        level = ((row // (2 * size)) == (col // (2 * size))) & ((row // size) != (col // size))
        masks.append(jnp.where(level, 1.0, 0.0).astype(BF16))
        size *= 2
    pad = jnp.zeros((8 - heads, STEP), F32)
    betas = jnp.transpose(jnp.concatenate([b_ref[...], pad], axis=0))
    work = {}
    for p in range(STEP // PAIR):
        rows = pl.ds(p * PAIR, PAIR)
        log = d_ref[rows, :]
        l1 = log.astype(BF16)
        r1 = log - l1.astype(F32)
        l2 = r1.astype(BF16)
        l3 = (r1 - l2.astype(F32)).astype(BF16)
        acc = mm(tri, l1) + (mm(tri, l2) + mm(tri, l3))
        top = lax.broadcasted_iota(jnp.int32, acc.shape, 0) < CH
        last = jnp.where(top, acc[CH - 1 : CH, :], acc[PAIR - 1 : PAIR, :])
        grow = jnp.exp(acc)
        shrink = jnp.exp(-acc)
        tail = jnp.exp(last - acc)
        total = jnp.exp(last)
        for h in range(heads):
            cols = pl.ds(h * 128, 128)
            hs = slice(h * 128, h * 128 + 128)
            key = unit(k_ref[rows, cols].astype(F32))
            query = unit(q_ref[rows, cols].astype(F32))
            beta = betas[p * PAIR : p * PAIR + PAIR, h : h + 1]
            key_hat = key * grow[:, hs]
            key_inv = key * shrink[:, hs]
            key_end = key * tail[:, hs]
            query_hat = query * grow[:, hs]
            low = jnp.where(strict, dot3(key_hat, key_inv, NT) * beta, 0.0)
            score = jnp.where(incl, dot1(query_hat, key_inv, NT), 0.0)
            right = jnp.concatenate([beta * key_hat, beta * v_ref[rows, cols].astype(F32)], axis=1)
            work[p, h] = (low, right, score, query_hat, key_end, total[:, hs])
    invs = {at: eye - jnp.where(first, work[at][0], 0.0) for at in work}
    parts = {at: work[at][0].astype(BF16) for at in work}
    for mask in masks:
        held = {at: invs[at].astype(BF16) for at in work}
        steps = {at: mm(parts[at] * mask, held[at]).astype(BF16) for at in work}
        for at in work:
            invs[at] = invs[at] - mm(held[at], steps[at])
    rest = {at: eye - invs[at] - dot3(work[at][0], invs[at]) for at in work}
    for at in work:
        invs[at] = invs[at] + dot1(invs[at], rest[at])
    for at in work:
        work[at] = (dot3(invs[at], work[at][1]),) + work[at][2:]
    zero = jnp.zeros((CH, 128), F32)
    cur = [state[h] for h in range(heads)]
    for p in range(STEP // PAIR):
        for half in range(2):
            rs = slice(half * CH, half * CH + CH)
            at = pl.ds(p * PAIR + half * CH, CH)
            leads = []
            for h in range(heads):
                solved, score, query_hat, key_end, total = work[p, h]
                leads.append(dot3(jnp.concatenate([solved[rs, :128], query_hat[rs]], axis=0), cur[h]))
            for h in range(heads):
                solved, score, query_hat, key_end, total = work[p, h]
                upd = jnp.concatenate([zero, solved[rs, 128:]], axis=1) - leads[h][:CH]
                fade = jnp.transpose(total[half * CH : half * CH + 8, :])[:, :1]
                cur[h] = fade * cur[h] + dot3(key_end[rs], upd, TN)
                out = leads[h][CH:] + dot1(score[rs, rs], upd)
                qo_ref[at, h * 128 : h * 128 + 128] = out[:, :128].astype(qo_ref.dtype)
                oo_ref[at, h * 128 : h * 128 + 128] = out[:, 128:]
    for h in range(heads):
        state[h] = cur[h]

    @pl.when(step == pl.num_programs(0) - 1)
    def _():
        for h in range(heads):
            mb_ref[h] = state[h].astype(mb_ref.dtype)


def delta(q, k, v, d, bt):
    rows, width = q.shape
    heads = width // 128
    spec = pl.BlockSpec((STEP, width), lambda i: (i, 0))
    return pl.pallas_call(
        delta_kernel,
        grid=(rows // STEP,),
        out_shape=(
            jax.ShapeDtypeStruct((rows, width), BF16),
            jax.ShapeDtypeStruct((rows, width), F32),
            jax.ShapeDtypeStruct((heads, 128, 256), BF16),
        ),
        in_specs=[spec, spec, spec, spec, pl.BlockSpec((heads, STEP), lambda i: (0, i))],
        out_specs=(spec, spec, pl.BlockSpec((heads, 128, 256), lambda i: (0, 0, 0))),
        scratch_shapes=[pltpu.VMEM((heads, 128, 256), F32)],
        compiler_params=pltpu.CompilerParams(vmem_limit_bytes=60 * 2**20),
        cost_estimate=pl.CostEstimate(flops=5_000_000_000, bytes_accessed=6_000_000, transcendentals=0),
        name="delta_chunks",
    )(q, k, v, d, bt)


def mixer_stage(
    mb_ref, q_any, o_any, gate_any, resid_any, gain_ref, w_any, hidden_ref, normed_ref,
    near, far, total, enter, mixed, mix, wide, q_ref, o_ref, gate_ref, resid_ref,
    enter_s, near_s, near_r, far_s, far_r, mix_s, mix_r, fetch_s, share_s, share_r, ring_s, ring_r, later,
):
    heads = mb_ref.shape[0]
    seq, exp = lax.axis_index("seq"), lax.axis_index("exp")
    group, slot, core = seq // NEAR, seq % NEAR, seq % 2
    exps = mix.shape[0]
    rows = normed_ref.shape[0]
    pairs = ((w_any.at[pl.ds(pl.multiple_of(core * 128, 128), 128)], wide.at[core, exp]), (q_any, q_ref), (o_any, o_ref), (gate_any, gate_ref), (resid_any, resid_ref))
    fetches = [pltpu.make_async_copy(source, kept, fetch_s.at[i]) for i, (source, kept) in enumerate(pairs)]
    for fetch in fetches:
        fetch.start()

    reach = (exps // 2, exps // 2 - 1)

    def w_copy(way, step):
        ahead = 1 - 2 * way
        view = wide.at[core, (exp + exps - ahead * step) % exps]
        return pltpu.make_async_remote_copy(
            src_ref=view, dst_ref=view, send_sem=ring_s, recv_sem=ring_r.at[way, step],
            device_id={"exp": (exp + exps + ahead) % exps}, device_id_type=MESH)

    def share(block):
        view = wide.at[core, block]
        pltpu.make_async_remote_copy(
            src_ref=view, dst_ref=view, send_sem=share_s, recv_sem=share_r,
            device_id={"seq": seq + 1 - 2 * core}, device_id_type=MESH).start()

    def advance(step):
        for way in range(2):
            if step <= reach[way]:
                block = (exp + exps - (1 - 2 * way) * step) % exps
                view = wide.at[core, block]
                pltpu.make_async_copy(view, view, ring_r.at[way, step - 1]).wait()
                if step < reach[way]:
                    w_copy(way, step).start()
                share(block)

    def near_copy(peer, place):
        return pltpu.make_async_remote_copy(
            src_ref=mb_ref.at[peer % 2], dst_ref=near.at[place], send_sem=near_s.at[peer], recv_sem=near_r.at[place],
            device_id={"seq": group * NEAR + peer}, device_id_type=MESH)

    def far_copy(peer, place):
        return pltpu.make_async_remote_copy(
            src_ref=total, dst_ref=far.at[place], send_sem=far_s.at[peer], recv_sem=far_r.at[place],
            device_id={"seq": peer * NEAR + slot}, device_id_type=MESH)

    def mix_copy(peer, place):
        return pltpu.make_async_remote_copy(
            src_ref=mixed.at[peer], dst_ref=mix.at[place], send_sem=mix_s.at[peer], recv_sem=mix_r.at[place],
            device_id={"exp": peer}, device_id_type=MESH)

    for d in range(1, NEAR):
        near_copy((slot + d) % NEAR, slot).start()
    near[slot] = mb_ref[core]
    for fetch in fetches:
        fetch.wait()
    w_copy(0, 0).start()
    w_copy(1, 0).start()
    share(exp)
    for fetch in later:
        fetch.start()
    row = lax.broadcasted_iota(jnp.int32, (128, 256), 0)
    col = lax.broadcasted_iota(jnp.int32, (128, 256), 1)
    start = jnp.where(row == col, 1.0, 0.0).astype(F32)
    shifts = col >= 128

    def apply(block, carried):
        high, low = split(carried)
        lead = block[:, :128]
        return mm(lead, high) + mm(lead, low)

    cur, even, odd = start, start, start
    for j in range(NEAR):
        @pl.when(j != slot)
        def _():
            near_copy(j, j).wait_recv()

        if j % 2:
            odd = jnp.where(slot // 2 == j // 2, cur, odd)
        else:
            even = jnp.where(slot // 2 == j // 2, cur, even)
        block = near[j]
        cur = apply(block, cur) + jnp.where(shifts, block.astype(F32), 0.0)
        if j == 3:
            advance(1)
    total[...] = cur.astype(BF16)
    for d in range(1, FAR):
        far_copy((group + d) % FAR, group).start()
    far[group] = total[...]
    advance(2)
    state = jnp.zeros((128, 128), F32)
    for g in range(FAR):
        @pl.when(g != group)
        def _():
            far_copy(g, g).wait_recv()

        block = far[g]
        state = jnp.where(g < group, apply(block, state) + block[:, 128:].astype(F32), state)
    first = dot3(even[:, :128], state) + even[:, 128:]
    second = dot3(odd[:, :128], state) + odd[:, 128:]
    enter[0] = jnp.where(core == 0, second, first).astype(BF16)
    hand = pltpu.make_async_remote_copy(
        src_ref=enter.at[0], dst_ref=enter.at[1], send_sem=enter_s.at[0], recv_sem=enter_s.at[1],
        device_id={"seq": seq + 1 - 2 * core}, device_id_type=MESH)
    hand.start()
    advance(3)
    mine = jnp.where(core == 0, first, second)
    hand.wait()
    theirs = enter[1].astype(F32)
    parts = [split(jnp.where(core == h, mine, theirs)) for h in range(heads)]

    def mix_rows(peer):
        at = pl.ds(pl.multiple_of(peer * rows, rows), rows)
        for h in range(heads):
            cols = pl.ds(h * 128, 128)
            query = q_ref[at, cols]
            out = mm(query, parts[h][0]) + mm(query, parts[h][1]) + o_ref[at, cols]
            out = out * lax.rsqrt(jnp.mean(out * out, axis=-1, keepdims=True) + epsilon)
            gate = gate_ref[at, cols].astype(F32)
            mixed[peer, :, cols] = (out / (1.0 + jnp.exp(-gate))).astype(BF16)

    for d in range(1, exps):
        peer = (exp + d) % exps
        mix_rows(peer)
        mix_copy(peer, exp).start()
    mix_rows(exp)
    mix[exp] = mixed[exp]
    advance(4)
    pltpu.make_async_copy(wide.at[1 - core], wide.at[1 - core], share_r).wait()
    acc = resid_ref[...].astype(F32)
    for d in range(exps):
        source = (exp + exps - d) % exps
        if d:
            mix_copy(source, source).wait_recv()
        for h in range(heads):
            acc = acc + mm(mix[source, :, h * 128 : h * 128 + 128], wide[h, source])
    hidden_ref[...] = acc
    scale = lax.rsqrt(jnp.mean(acc * acc, axis=-1, keepdims=True) + epsilon)
    normed_ref[...] = (acc * scale * gain_ref[...].reshape(1, -1)).astype(BF16)
    for d in range(1, NEAR):
        near_copy((slot + d) % NEAR, slot).wait_send()
    for d in range(1, FAR):
        far_copy((group + d) % FAR, group).wait_send()
    for d in range(1, exps):
        mix_copy((exp + d) % exps, exp).wait_send()
    pltpu.make_async_copy(wide.at[core], wide.at[core], share_s).wait()
    sent = wide.at[core, pl.ds(0, exps - 1)]
    pltpu.make_async_copy(sent, sent, ring_s).wait()


def expert_kernel(
    mb_ref, q_any, o_any, gate_any, resid_any, gain_ref, w_any, table_ref, router_any, wgu_ref, wd_ref, out_ref,
    hidden_ref, normed_ref, router_ref, near, far, total, enter, mixed, mix, wide, q_ref, o_ref, gate_ref, resid_ref,
    enter_s, near_s, near_r, far_s, far_r, mix_s, mix_r, mixer_s, share_s, share_r, ring_s, ring_r, spread, landed, final, own, every, leave, arrive, inner, back, home, give, take, wgu, wd,
    fetch_s, spread_s, spread_r, every_s, every_r, leave_s, leave_r, back_s, back_r, give_s, give_r, end_s, end_r,
):
    seq, exp = lax.axis_index("seq"), lax.axis_index("exp")
    seqs, exps = lax.axis_size("seq"), lax.axis_size("exp")
    width = out_ref.shape[1]
    third = width // 3
    parts = every.shape[0]
    group = every.shape[2]
    hidden_width = wd.shape[0]
    core, across, along = seq % 2, (seq // 2) % 4, seq // 8
    load_up = pltpu.make_async_copy(wgu_ref, wgu, fetch_s.at[0])
    load_down = pltpu.make_async_copy(wd_ref, wd, fetch_s.at[1])
    load_router = pltpu.make_async_copy(router_any, router_ref, fetch_s.at[2])

    def plane(p):
        step = p % 16
        turn = 1 + 2 * core
        dx = (step % 4) * turn
        dy = ((step // 4 + step) % 4) * turn
        return ((along + dy) % 4) * 8 + ((across + dx) % 4) * 2 + (core + p // 16) % 2

    def column(d):
        return (exp + d) % exps

    barrier = pltpu.get_barrier_semaphore()

    @pl.loop(1, seqs)
    def _(p):
        pl.semaphore_signal(barrier, inc=1, device_id={"seq": plane(p)}, device_id_type=MESH)

    @pl.loop(1, exps)
    def _(d):
        pl.semaphore_signal(barrier, inc=1, device_id={"exp": column(d)}, device_id_type=MESH)

    pl.semaphore_wait(barrier, seqs + exps - 2)
    mixer_stage(
        mb_ref, q_any, o_any, gate_any, resid_any, gain_ref, w_any, hidden_ref, normed_ref,
        near, far, total, enter, mixed, mix, wide, q_ref, o_ref, gate_ref, resid_ref,
        enter_s, near_s, near_r, far_s, far_r, mix_s, mix_r, mixer_s, share_s, share_r, ring_s, ring_r, (load_router, load_up, load_down))

    row = lax.broadcasted_iota(jnp.int32, (512, 128), 0)
    col = lax.broadcasted_iota(jnp.int32, (512, 128), 1)
    place = (row % 16) // 4 * 32 + row // 16 == col
    to_wire = [jnp.where(place & (row % 4 == g), 1.0, 0.0).astype(BF16) for g in range(3)]
    row = lax.broadcasted_iota(jnp.int32, (128, 512), 0)
    col = lax.broadcasted_iota(jnp.int32, (128, 512), 1)
    place = (col % 16) // 4 * 32 + col // 16 == row
    from_wire = [jnp.where(place & (col % 4 == g), 1.0, 0.0).astype(BF16) for g in range(3)]

    def lay_out(rows):
        total = mm(to_wire[0], rows[:, :third])
        total = total + mm(to_wire[1], rows[:, third : 2 * third])
        total = total + mm(to_wire[2], rows[:, 2 * third :])
        spread[...] = total.astype(BF16)

    def wire(peer, place, target, send, recv):
        return pltpu.make_async_remote_copy(
            src_ref=spread.at[pl.ds(pl.multiple_of(peer * 16, 16), 16)],
            dst_ref=target.at[pl.ds(pl.multiple_of(place * 16, 16), 16)],
            send_sem=send, recv_sem=recv, device_id={"seq": peer}, device_id_type=MESH)

    def slots(source, target, part, peer, place, send, recv):
        return pltpu.make_async_remote_copy(
            src_ref=source.at[part, pl.ds(pl.multiple_of(peer * 16, 16), 16)],
            dst_ref=target.at[part, pl.ds(pl.multiple_of(place * 16, 16), 16)],
            send_sem=send.at[part], recv_sem=recv.at[part], device_id={"seq": peer}, device_id_type=MESH)

    def settle(view, sem):
        pltpu.make_async_copy(view, view, sem).wait()

    others = (seqs - 1) * 16
    mine = pl.ds(pl.multiple_of(seq * 16, 16), 16)

    lay_out(normed_ref[...])

    @pl.loop(1, seqs)
    def _(p):
        wire(plane(p), seq, landed, spread_s, spread_r).start()

    landed[mine] = spread[mine]

    load_router.wait()
    count = table_ref.shape[0]
    row = lax.broadcasted_iota(jnp.int32, (count, count), 0)
    col = lax.broadcasted_iota(jnp.int32, (count, count), 1)
    order = jnp.where(row == (col % seqs) * exps + col // seqs, 1.0, 0.0).astype(BF16)
    table = mm(table_ref[...].astype(F32).astype(BF16), order, TN)
    lane = lax.broadcasted_iota(jnp.int32, table.shape, 1)
    sub = lax.broadcasted_iota(jnp.int32, table.shape, 0)
    target = jnp.floor(jnp.sum(jnp.where(sub == exp, table, 0.0), axis=0, keepdims=True) / exps)
    hits = lax.broadcasted_iota(jnp.int32, (seqs, 256), 0).astype(F32) == target
    before = lax.broadcasted_iota(jnp.int32, (256, 256), 0) < lax.broadcasted_iota(jnp.int32, (256, 256), 1)
    counts = mm(jnp.where(hits, 1.0, 0.0).astype(BF16), jnp.where(before, 1.0, 0.0).astype(BF16))
    rank = jnp.sum(jnp.where(hits, counts, 0.0), axis=0, keepdims=True)
    goal = target * 16.0 + rank
    pick = jnp.where(lax.broadcasted_iota(jnp.int32, (512, 256), 0).astype(F32) == goal, 1.0, 0.0)
    unpick = jnp.transpose(pick).astype(BF16)
    pick = pick.astype(BF16)
    ids = jnp.sum(jnp.where(lane == exp * seqs + seq, table, 0.0), axis=1, keepdims=True)
    chosen = jnp.sum(jnp.where(lane.astype(F32) == ids, 1.0, 0.0), axis=0, keepdims=True)
    scores = mm(normed_ref[...], router_ref[...])
    denom = jnp.sum(chosen / (1.0 + jnp.exp(-scores)), axis=1, keepdims=True)
    here = lax.broadcasted_iota(jnp.int32, (256, 128), 0) == seq * exps + exp
    router_col = mm(router_ref[...], jnp.where(here, 1.0, 0.0).astype(BF16)).astype(BF16)

    settle(landed.at[pl.ds(0, others)], spread_r)
    settle(spread.at[pl.ds(0, others)], spread_s)
    for g in range(3):
        own[:, g * third : (g + 1) * third] = mm(from_wire[g], landed[...]).astype(BF16)

    def ring(part, way, step):
        ahead = 1 - 2 * way
        block = (exp + exps - ahead * step) % exps
        return pltpu.make_async_remote_copy(
            src_ref=every.at[part, block], dst_ref=every.at[part, block],
            send_sem=every_s.at[part], recv_sem=every_r.at[part, way, step],
            device_id={"exp": (exp + exps + ahead) % exps}, device_id_type=MESH)

    def ring_wait(part, way, step):
        block = (exp + exps - (1 - 2 * way) * (step + 1)) % exps
        view = every.at[part, block]
        pltpu.make_async_copy(view, view, every_r.at[part, way, step]).wait()

    half = exps // 2
    for wave in range(parts + half):
        for part in range(parts):
            step = wave - part
            for way in range(2):
                if 0 <= step < half - (part + way) % 2:
                    if step == 0 and way == 0:
                        every[part, exp] = own[part * group : part * group + group]
                    if step:
                        ring_wait(part, way, step - 1)
                    ring(part, way, step).start()
        part = wave - half
        if part >= 0:
            for way in range(2):
                ring_wait(part, way, half - 1 - (part + way) % 2)
            rows = every[part].reshape(exps * group, width)
            leave[part] = mm(pick, rows).astype(BF16)

            @pl.loop(1, seqs)
            def _(p):
                slots(leave, arrive, part, plane(p), seq, leave_s, leave_r).start()

            arrive[part, mine] = leave[part, mine]

    load_up.wait()
    load_down.wait()

    @pl.loop(0, parts)
    def _(part):
        settle(arrive.at[part, pl.ds(0, others)], leave_r.at[part])
        score = 1.0 / (1.0 + jnp.exp(-mm(arrive[part], router_col)))

        @pl.loop(0, hidden_width // 256)
        def _(j):
            rows = arrive[part]
            left = mm(rows, wgu[:, pl.ds(pl.multiple_of(j * 256, 256), 256)])
            right = mm(rows, wgu[:, pl.ds(pl.multiple_of(hidden_width + j * 256, 256), 256)])
            inner[:, pl.ds(pl.multiple_of(j * 256, 256), 256)] = (left / (1.0 + jnp.exp(-left)) * right).astype(BF16)

        weight = jnp.concatenate([score] * 3, axis=1)
        for g in range(3):
            cols = pl.ds(g * third, third)
            back[part, :, cols] = (weight * mm(inner[...], wd[:, cols])).astype(BF16)

        @pl.loop(1, seqs)
        def _(p):
            slots(back, home, part, plane(p), seq, back_s, back_r).start()

        home[part, mine] = back[part, mine]

    def deliver(part, peer, place):
        return pltpu.make_async_remote_copy(
            src_ref=give.at[part, peer], dst_ref=take.at[part, place],
            send_sem=give_s.at[part], recv_sem=give_r.at[part], device_id={"exp": peer}, device_id_type=MESH)

    @pl.loop(0, parts)
    def _(part):
        settle(home.at[part, pl.ds(0, others)], back_r.at[part])
        give[part] = mm(unpick, home[part]).astype(BF16).reshape(exps, group, width)

        @pl.loop(1, exps)
        def _(d):
            deliver(part, column(d), exp).start()

        take[part, exp] = give[part, exp]

    @pl.loop(0, parts)
    def _(part):
        settle(take.at[part, pl.ds(0, exps - 1)], give_r.at[part])
        own_rows = pl.ds(pl.multiple_of(part * group, group), group)
        settle(every.at[part, pl.ds(0, exps - 1)], every_s.at[part])
        total = take[part, 0].astype(F32)
        for c in range(1, exps):
            total = total + take[part, c].astype(F32)
        own[own_rows] = total.astype(BF16)

    lay_out(own[...])

    @pl.loop(1, seqs)
    def _(p):
        wire(plane(p), seq, final, end_s, end_r).start()

    final[mine] = spread[mine]
    settle(final.at[pl.ds(0, others)], end_r)
    scale = route_scale / denom
    for g in range(3):
        cols = pl.ds(g * third, third)
        out_ref[:, cols] = (hidden_ref[:, cols] + scale * mm(from_wire[g], final[...])).astype(BF16)
    settle(spread.at[pl.ds(0, others)], end_s)

    @pl.loop(0, parts)
    def _(part):
        settle(leave.at[part, pl.ds(0, others)], leave_s.at[part])
        settle(back.at[part, pl.ds(0, others)], back_s.at[part])
        settle(give.at[part, pl.ds(0, exps - 1)], give_s.at[part])


def experts(mb, q, o, gate, resid, gain, w_out, table, router, wgu, wd, seqs, exps):
    rows, width = resid.shape
    heads = mb.shape[0]
    parts, group = rows // seqs, seqs
    held = seqs * 16
    vmem = pl.BlockSpec(memory_space=pltpu.VMEM)
    hbm = pl.BlockSpec(memory_space=pl.ANY)
    dma = pltpu.SemaphoreType.DMA
    slots = pltpu.VMEM((parts, held, width), BF16)
    blocks = pltpu.VMEM((parts, exps, group, width), BF16)
    small = pltpu.VMEM((held, width // 3), BF16)
    mixes = pltpu.VMEM((exps, rows, heads * 128), BF16)
    return pl.pallas_call(
        expert_kernel,
        out_shape=jax.ShapeDtypeStruct((rows, width), BF16),
        in_specs=[vmem] + [hbm] * 4 + [vmem, hbm, vmem] + [hbm] * 3,
        out_specs=vmem,
        scratch_shapes=[
            pltpu.VMEM((rows, width), F32), pltpu.VMEM((rows, width), BF16), pltpu.VMEM(router.shape, BF16),
            pltpu.VMEM((NEAR, 128, 256), BF16), pltpu.VMEM((FAR, 128, 256), BF16),
            pltpu.VMEM((128, 256), BF16), pltpu.VMEM((2, 128, 128), BF16), mixes, mixes, pltpu.VMEM((2, exps, 128, width), BF16),
            pltpu.VMEM(q.shape, BF16), pltpu.VMEM(o.shape, F32), pltpu.VMEM(gate.shape, BF16),
            pltpu.VMEM(resid.shape, BF16),
            dma((2,)), dma((NEAR,)), dma((NEAR,)), dma((FAR,)), dma((FAR,)), dma((exps,)), dma((exps,)), dma((5,)), dma, dma, dma, dma((2, exps // 2)),
            small, small, small, pltpu.VMEM((rows, width), BF16),
            blocks, slots, slots, pltpu.VMEM((held, wd.shape[0]), BF16), slots, slots, blocks, blocks,
            pltpu.VMEM(wgu.shape, BF16), pltpu.VMEM(wd.shape, BF16),
            dma((3,)), dma, dma, dma((parts,)), dma((parts, 2, exps // 2)), dma((parts,)), dma((parts,)),
            dma((parts,)), dma((parts,)), dma((parts,)), dma((parts,)), dma, dma,
        ],
        compiler_params=pltpu.CompilerParams(
            collective_id=0, has_side_effects=True, vmem_limit_bytes=58 * 2**20
        ),
        name="mix_and_experts",
    )(mb, q, o, gate, resid, gain, w_out, table, router, wgu, wd)


def local(
    queries,
    keys,
    values,
    out_gate,
    decay_log,
    beta,
    w_out,
    resid,
    norm_gain,
    router,
    w_gate_up,
    w_down,
    block_experts,
):
    seq_count = lax.axis_size("seq")
    exp_count = lax.axis_size("exp")
    q_lead, o_lead, carried = delta(queries, keys, values, decay_log, beta)
    return experts(
        carried, q_lead, o_lead, out_gate, resid, norm_gain, w_out,
        block_experts, router, w_gate_up[0], w_down[0], seq_count, exp_count,
    )


def solution(mesh):
    return jax.shard_map(
        local,
        mesh=mesh,
        in_specs=(
            P("seq", "exp"),
            P("seq", "exp"),
            P("seq", "exp"),
            P("seq", "exp"),
            P("seq", "exp"),
            P("exp", "seq"),
            P("exp", None),
            P(("seq", "exp"), None),
            P(),
            P(),
            P(("seq", "exp"), None, None),
            P(("seq", "exp"), None, None),
            P(),
        ),
        out_specs=P(("seq", "exp"), None),
        check_vma=False,
    )
```

```python
import functools

import jax
import jax.numpy as jnp
from jax import lax
from jax.experimental import pallas as pl
from jax.experimental.pallas import tpu as pltpu
from jax.sharding import PartitionSpec as P

DK = 128
TOPK = 8
CH = 64
PAIR = 128
STEP = 512
NEAR = 8
FAR = 4
F32, BF16 = jnp.float32, jnp.bfloat16
MESH = pl.DeviceIdType.MESH
NN = (((1,), (0,)), ((), ()))
NT = (((1,), (1,)), ((), ()))
TN = (((0,), (0,)), ((), ()))

route_scale = 2.446
epsilon = 1e-06


def split(a):
    high = a.astype(BF16)
    return high, (a - high.astype(F32)).astype(BF16)


def mm(a, b, dims=NN):
    return lax.dot_general(a, b, dims, preferred_element_type=F32)


def dot1(a, b, dims=NN):
    return mm(a.astype(BF16), b.astype(BF16), dims)


def dot3(a, b, dims=NN):
    ah, al = split(a)
    bh, bl = split(b)
    return mm(ah, bh, dims) + (mm(ah, bl, dims) + mm(al, bh, dims))


def unit(x):
    return x * lax.rsqrt(jnp.sum(x * x, axis=-1, keepdims=True) + epsilon)


def delta_kernel(q_ref, k_ref, v_ref, d_ref, b_ref, qo_ref, oo_ref, mb_ref, state):
    heads = q_ref.shape[1] // 128
    step = pl.program_id(0)
    row = lax.broadcasted_iota(jnp.int32, (PAIR, PAIR), 0)
    col = lax.broadcasted_iota(jnp.int32, (PAIR, PAIR), 1)

    @pl.when(step == 0)
    def _():
        eye = jnp.where(row == col, 1.0, 0.0).astype(F32)
        for h in range(heads):
            state[h, :, :128] = eye
            state[h, :, 128:] = jnp.zeros((128, 128), F32)

    same = (row // CH) == (col // CH)
    incl = same & (col <= row)
    strict = same & (col < row)
    tri = jnp.where(incl, 1.0, 0.0).astype(BF16)
    eye = jnp.where(row == col, 1.0, 0.0).astype(F32)
    first = (row // 2) == (col // 2)
    masks = []
    size = 2
    while size < CH:
        level = ((row // (2 * size)) == (col // (2 * size))) & ((row // size) != (col // size))
        masks.append(jnp.where(level, 1.0, 0.0).astype(BF16))
        size *= 2
    pad = jnp.zeros((8 - heads, STEP), F32)
    betas = jnp.transpose(jnp.concatenate([b_ref[...], pad], axis=0))
    work = {}
    for p in range(STEP // PAIR):
        rows = pl.ds(p * PAIR, PAIR)
        log = d_ref[rows, :]
        l1 = log.astype(BF16)
        r1 = log - l1.astype(F32)
        l2 = r1.astype(BF16)
        l3 = (r1 - l2.astype(F32)).astype(BF16)
        acc = mm(tri, l1) + (mm(tri, l2) + mm(tri, l3))
        top = lax.broadcasted_iota(jnp.int32, acc.shape, 0) < CH
        last = jnp.where(top, acc[CH - 1 : CH, :], acc[PAIR - 1 : PAIR, :])
        grow = jnp.exp(acc)
        shrink = jnp.exp(-acc)
        tail = jnp.exp(last - acc)
        total = jnp.exp(last)
        for h in range(heads):
            cols = pl.ds(h * 128, 128)
            hs = slice(h * 128, h * 128 + 128)
            key = unit(k_ref[rows, cols].astype(F32))
            query = unit(q_ref[rows, cols].astype(F32))
            beta = betas[p * PAIR : p * PAIR + PAIR, h : h + 1]
            key_hat = key * grow[:, hs]
            key_inv = key * shrink[:, hs]
            key_end = key * tail[:, hs]
            query_hat = query * grow[:, hs]
            low = jnp.where(strict, dot3(key_hat, key_inv, NT) * beta, 0.0)
            score = jnp.where(incl, dot1(query_hat, key_inv, NT), 0.0)
            right = jnp.concatenate([beta * key_hat, beta * v_ref[rows, cols].astype(F32)], axis=1)
            work[p, h] = (low, right, score, query_hat, key_end, total[:, hs])
    invs = {at: eye - jnp.where(first, work[at][0], 0.0) for at in work}
    parts = {at: work[at][0].astype(BF16) for at in work}
    for mask in masks:
        held = {at: invs[at].astype(BF16) for at in work}
        steps = {at: mm(parts[at] * mask, held[at]).astype(BF16) for at in work}
        for at in work:
            invs[at] = invs[at] - mm(held[at], steps[at])
    rest = {at: eye - invs[at] - dot3(work[at][0], invs[at]) for at in work}
    for at in work:
        invs[at] = invs[at] + dot1(invs[at], rest[at])
    for at in work:
        work[at] = (dot3(invs[at], work[at][1]),) + work[at][2:]
    zero = jnp.zeros((CH, 128), F32)
    cur = [state[h] for h in range(heads)]
    for p in range(STEP // PAIR):
        for half in range(2):
            rs = slice(half * CH, half * CH + CH)
            at = pl.ds(p * PAIR + half * CH, CH)
            leads = []
            for h in range(heads):
                solved, score, query_hat, key_end, total = work[p, h]
                leads.append(dot3(jnp.concatenate([solved[rs, :128], query_hat[rs]], axis=0), cur[h]))
            for h in range(heads):
                solved, score, query_hat, key_end, total = work[p, h]
                upd = jnp.concatenate([zero, solved[rs, 128:]], axis=1) - leads[h][:CH]
                fade = jnp.transpose(total[half * CH : half * CH + 8, :])[:, :1]
                cur[h] = fade * cur[h] + dot3(key_end[rs], upd, TN)
                out = leads[h][CH:] + dot1(score[rs, rs], upd)
                qo_ref[at, h * 128 : h * 128 + 128] = out[:, :128].astype(qo_ref.dtype)
                oo_ref[at, h * 128 : h * 128 + 128] = out[:, 128:]
    for h in range(heads):
        state[h] = cur[h]

    @pl.when(step == pl.num_programs(0) - 1)
    def _():
        for h in range(heads):
            mb_ref[h] = state[h].astype(mb_ref.dtype)


def delta(q, k, v, d, bt):
    rows, width = q.shape
    heads = width // 128
    spec = pl.BlockSpec((STEP, width), lambda i: (i, 0))
    return pl.pallas_call(
        delta_kernel,
        grid=(rows // STEP,),
        out_shape=(
            jax.ShapeDtypeStruct((rows, width), BF16),
            jax.ShapeDtypeStruct((rows, width), F32),
            jax.ShapeDtypeStruct((heads, 128, 256), BF16),
        ),
        in_specs=[spec, spec, spec, spec, pl.BlockSpec((heads, STEP), lambda i: (0, i))],
        out_specs=(spec, spec, pl.BlockSpec((heads, 128, 256), lambda i: (0, 0, 0))),
        scratch_shapes=[pltpu.VMEM((heads, 128, 256), F32)],
        compiler_params=pltpu.CompilerParams(vmem_limit_bytes=60 * 2**20),
        cost_estimate=pl.CostEstimate(flops=5_000_000_000, bytes_accessed=6_000_000, transcendentals=0),
        name="delta_chunks",
    )(q, k, v, d, bt)


def mixer_stage(
    mb_ref, q_any, o_any, gate_any, resid_any, gain_ref, w_any, hidden_ref, normed_ref,
    near, far, total, enter, mixed, mix, wide, q_ref, o_ref, gate_ref, resid_ref,
    enter_s, near_s, near_r, far_s, far_r, mix_s, mix_r, fetch_s, share_s, share_r, ring_s, ring_r, later,
):
    heads = mb_ref.shape[0]
    seq, exp = lax.axis_index("seq"), lax.axis_index("exp")
    group, slot, core = seq // NEAR, seq % NEAR, seq % 2
    exps = mix.shape[0]
    rows = normed_ref.shape[0]
    pairs = ((w_any.at[pl.ds(pl.multiple_of(core * 128, 128), 128)], wide.at[core, exp]), (q_any, q_ref), (o_any, o_ref), (gate_any, gate_ref), (resid_any, resid_ref))
    fetches = [pltpu.make_async_copy(source, kept, fetch_s.at[i]) for i, (source, kept) in enumerate(pairs)]
    for fetch in fetches:
        fetch.start()

    reach = (exps // 2, exps // 2 - 1)

    def w_copy(way, step):
        ahead = 1 - 2 * way
        view = wide.at[core, (exp + exps - ahead * step) % exps]
        return pltpu.make_async_remote_copy(
            src_ref=view, dst_ref=view, send_sem=ring_s, recv_sem=ring_r.at[way, step],
            device_id={"exp": (exp + exps + ahead) % exps}, device_id_type=MESH)

    def share(block):
        view = wide.at[core, block]
        pltpu.make_async_remote_copy(
            src_ref=view, dst_ref=view, send_sem=share_s, recv_sem=share_r,
            device_id={"seq": seq + 1 - 2 * core}, device_id_type=MESH).start()

    def advance(step):
        for way in range(2):
            if step <= reach[way]:
                block = (exp + exps - (1 - 2 * way) * step) % exps
                view = wide.at[core, block]
                pltpu.make_async_copy(view, view, ring_r.at[way, step - 1]).wait()
                if step < reach[way]:
                    w_copy(way, step).start()
                share(block)

    def near_copy(peer, place):
        return pltpu.make_async_remote_copy(
            src_ref=mb_ref.at[peer % 2], dst_ref=near.at[place], send_sem=near_s.at[peer], recv_sem=near_r.at[place],
            device_id={"seq": group * NEAR + peer}, device_id_type=MESH)

    def far_copy(peer, place):
        return pltpu.make_async_remote_copy(
            src_ref=total, dst_ref=far.at[place], send_sem=far_s.at[peer], recv_sem=far_r.at[place],
            device_id={"seq": peer * NEAR + slot}, device_id_type=MESH)

    def mix_copy(peer, place):
        return pltpu.make_async_remote_copy(
            src_ref=mixed.at[peer], dst_ref=mix.at[place], send_sem=mix_s.at[peer], recv_sem=mix_r.at[place],
            device_id={"exp": peer}, device_id_type=MESH)

    for d in range(1, NEAR):
        near_copy((slot + d) % NEAR, slot).start()
    near[slot] = mb_ref[core]
    for fetch in fetches:
        fetch.wait()
    w_copy(0, 0).start()
    w_copy(1, 0).start()
    share(exp)
    for fetch in later:
        fetch.start()
    row = lax.broadcasted_iota(jnp.int32, (128, 256), 0)
    col = lax.broadcasted_iota(jnp.int32, (128, 256), 1)
    start = jnp.where(row == col, 1.0, 0.0).astype(F32)
    shifts = col >= 128

    def apply(block, carried):
        high, low = split(carried)
        lead = block[:, :128]
        return mm(lead, high) + mm(lead, low)

    cur, even, odd = start, start, start
    for j in range(NEAR):
        @pl.when(j != slot)
        def _():
            near_copy(j, j).wait_recv()

        if j % 2:
            odd = jnp.where(slot // 2 == j // 2, cur, odd)
        else:
            even = jnp.where(slot // 2 == j // 2, cur, even)
        block = near[j]
        cur = apply(block, cur) + jnp.where(shifts, block.astype(F32), 0.0)
        if j == 3:
            advance(1)
    total[...] = cur.astype(BF16)
    for d in range(1, FAR):
        far_copy((group + d) % FAR, group).start()
    far[group] = total[...]
    advance(2)
    state = jnp.zeros((128, 128), F32)
    for g in range(FAR):
        @pl.when(g != group)
        def _():
            far_copy(g, g).wait_recv()

        block = far[g]
        state = jnp.where(g < group, apply(block, state) + block[:, 128:].astype(F32), state)
    first = dot3(even[:, :128], state) + even[:, 128:]
    second = dot3(odd[:, :128], state) + odd[:, 128:]
    enter[0] = jnp.where(core == 0, second, first).astype(BF16)
    hand = pltpu.make_async_remote_copy(
        src_ref=enter.at[0], dst_ref=enter.at[1], send_sem=enter_s.at[0], recv_sem=enter_s.at[1],
        device_id={"seq": seq + 1 - 2 * core}, device_id_type=MESH)
    hand.start()
    advance(3)
    mine = jnp.where(core == 0, first, second)
    hand.wait()
    theirs = enter[1].astype(F32)
    parts = [split(jnp.where(core == h, mine, theirs)) for h in range(heads)]

    def mix_rows(peer):
        at = pl.ds(pl.multiple_of(peer * rows, rows), rows)
        for h in range(heads):
            cols = pl.ds(h * 128, 128)
            query = q_ref[at, cols]
            out = mm(query, parts[h][0]) + mm(query, parts[h][1]) + o_ref[at, cols]
            out = out * lax.rsqrt(jnp.mean(out * out, axis=-1, keepdims=True) + epsilon)
            gate = gate_ref[at, cols].astype(F32)
            mixed[peer, :, cols] = (out / (1.0 + jnp.exp(-gate))).astype(BF16)

    for d in range(1, exps):
        peer = (exp + d) % exps
        mix_rows(peer)
        mix_copy(peer, exp).start()
    mix_rows(exp)
    mix[exp] = mixed[exp]
    advance(4)
    pltpu.make_async_copy(wide.at[1 - core], wide.at[1 - core], share_r).wait()
    acc = resid_ref[...].astype(F32)
    for d in range(exps):
        source = (exp + exps - d) % exps
        if d:
            mix_copy(source, source).wait_recv()
        for h in range(heads):
            acc = acc + mm(mix[source, :, h * 128 : h * 128 + 128], wide[h, source])
    hidden_ref[...] = acc
    scale = lax.rsqrt(jnp.mean(acc * acc, axis=-1, keepdims=True) + epsilon)
    normed_ref[...] = (acc * scale * gain_ref[...].reshape(1, -1)).astype(BF16)
    for d in range(1, NEAR):
        near_copy((slot + d) % NEAR, slot).wait_send()
    for d in range(1, FAR):
        far_copy((group + d) % FAR, group).wait_send()
    for d in range(1, exps):
        mix_copy((exp + d) % exps, exp).wait_send()
    pltpu.make_async_copy(wide.at[core], wide.at[core], share_s).wait()
    sent = wide.at[core, pl.ds(0, exps - 1)]
    pltpu.make_async_copy(sent, sent, ring_s).wait()


def expert_kernel(
    mb_ref, q_any, o_any, gate_any, resid_any, gain_ref, w_any, table_ref, router_any, wgu_ref, wd_ref, out_ref,
    hidden_ref, normed_ref, router_ref, near, far, total, enter, mixed, mix, wide, q_ref, o_ref, gate_ref, resid_ref,
    enter_s, near_s, near_r, far_s, far_r, mix_s, mix_r, mixer_s, share_s, share_r, ring_s, ring_r, spread, landed, final, own, every, leave, arrive, inner, back, home, give, take, wgu, wd,
    fetch_s, spread_s, spread_r, every_s, every_r, leave_s, leave_r, back_s, back_r, give_s, give_r, end_s, end_r,
):
    seq, exp = lax.axis_index("seq"), lax.axis_index("exp")
    seqs, exps = lax.axis_size("seq"), lax.axis_size("exp")
    width = out_ref.shape[1]
    third = width // 3
    parts = every.shape[0]
    group = every.shape[2]
    hidden_width = wd.shape[0]
    core, across, along = seq % 2, (seq // 2) % 4, seq // 8
    load_up = pltpu.make_async_copy(wgu_ref, wgu, fetch_s.at[0])
    load_down = pltpu.make_async_copy(wd_ref, wd, fetch_s.at[1])
    load_router = pltpu.make_async_copy(router_any, router_ref, fetch_s.at[2])

    def plane(p):
        step = p % 16
        turn = 1 + 2 * core
        dx = (step % 4) * turn
        dy = ((step // 4 + step) % 4) * turn
        return ((along + dy) % 4) * 8 + ((across + dx) % 4) * 2 + (core + p // 16) % 2

    def column(d):
        return (exp + d) % exps

    barrier = pltpu.get_barrier_semaphore()

    @pl.loop(1, seqs)
    def _(p):
        pl.semaphore_signal(barrier, inc=1, device_id={"seq": plane(p)}, device_id_type=MESH)

    @pl.loop(1, exps)
    def _(d):
        pl.semaphore_signal(barrier, inc=1, device_id={"exp": column(d)}, device_id_type=MESH)

    pl.semaphore_wait(barrier, seqs + exps - 2)
    mixer_stage(
        mb_ref, q_any, o_any, gate_any, resid_any, gain_ref, w_any, hidden_ref, normed_ref,
        near, far, total, enter, mixed, mix, wide, q_ref, o_ref, gate_ref, resid_ref,
        enter_s, near_s, near_r, far_s, far_r, mix_s, mix_r, mixer_s, share_s, share_r, ring_s, ring_r, (load_router, load_up, load_down))

    row = lax.broadcasted_iota(jnp.int32, (512, 128), 0)
    col = lax.broadcasted_iota(jnp.int32, (512, 128), 1)
    place = (row % 16) // 4 * 32 + row // 16 == col
    to_wire = [jnp.where(place & (row % 4 == g), 1.0, 0.0).astype(BF16) for g in range(3)]
    row = lax.broadcasted_iota(jnp.int32, (128, 512), 0)
    col = lax.broadcasted_iota(jnp.int32, (128, 512), 1)
    place = (col % 16) // 4 * 32 + col // 16 == row
    from_wire = [jnp.where(place & (col % 4 == g), 1.0, 0.0).astype(BF16) for g in range(3)]

    def lay_out(rows):
        total = mm(to_wire[0], rows[:, :third])
        total = total + mm(to_wire[1], rows[:, third : 2 * third])
        total = total + mm(to_wire[2], rows[:, 2 * third :])
        spread[...] = total.astype(BF16)

    def wire(peer, place, target, send, recv):
        return pltpu.make_async_remote_copy(
            src_ref=spread.at[pl.ds(pl.multiple_of(peer * 16, 16), 16)],
            dst_ref=target.at[pl.ds(pl.multiple_of(place * 16, 16), 16)],
            send_sem=send, recv_sem=recv, device_id={"seq": peer}, device_id_type=MESH)

    def slots(source, target, part, peer, place, send, recv):
        return pltpu.make_async_remote_copy(
            src_ref=source.at[part, pl.ds(pl.multiple_of(peer * 16, 16), 16)],
            dst_ref=target.at[part, pl.ds(pl.multiple_of(place * 16, 16), 16)],
            send_sem=send.at[part], recv_sem=recv.at[part], device_id={"seq": peer}, device_id_type=MESH)

    def settle(view, sem):
        pltpu.make_async_copy(view, view, sem).wait()

    others = (seqs - 1) * 16
    mine = pl.ds(pl.multiple_of(seq * 16, 16), 16)

    lay_out(normed_ref[...])

    @pl.loop(1, seqs)
    def _(p):
        wire(plane(p), seq, landed, spread_s, spread_r).start()

    landed[mine] = spread[mine]

    load_router.wait()
    count = table_ref.shape[1]
    row = lax.broadcasted_iota(jnp.int32, (count, count), 0)
    col = lax.broadcasted_iota(jnp.int32, (count, count), 1)
    order = jnp.where(row == (col % seqs) * exps + col // seqs, 1.0, 0.0).astype(BF16)
    table = mm(table_ref[...].astype(F32).astype(BF16), order)
    lane = lax.broadcasted_iota(jnp.int32, table.shape, 1)
    sub = lax.broadcasted_iota(jnp.int32, table.shape, 0)
    target = jnp.floor(jnp.sum(jnp.where(sub == exp, table, 0.0), axis=0, keepdims=True) / exps)
    hits = lax.broadcasted_iota(jnp.int32, (seqs, 256), 0).astype(F32) == target
    before = lax.broadcasted_iota(jnp.int32, (256, 256), 0) < lax.broadcasted_iota(jnp.int32, (256, 256), 1)
    counts = mm(jnp.where(hits, 1.0, 0.0).astype(BF16), jnp.where(before, 1.0, 0.0).astype(BF16))
    rank = jnp.sum(jnp.where(hits, counts, 0.0), axis=0, keepdims=True)
    goal = target * 16.0 + rank
    pick = jnp.where(lax.broadcasted_iota(jnp.int32, (512, 256), 0).astype(F32) == goal, 1.0, 0.0)
    unpick = jnp.transpose(pick).astype(BF16)
    pick = pick.astype(BF16)
    ids = jnp.sum(jnp.where(lane == exp * seqs + seq, table, 0.0), axis=1, keepdims=True)
    chosen = jnp.sum(jnp.where(lane.astype(F32) == ids, 1.0, 0.0), axis=0, keepdims=True)
    scores = mm(normed_ref[...], router_ref[...])
    denom = jnp.sum(chosen / (1.0 + jnp.exp(-scores)), axis=1, keepdims=True)
    here = lax.broadcasted_iota(jnp.int32, (256, 128), 0) == seq * exps + exp
    router_col = mm(router_ref[...], jnp.where(here, 1.0, 0.0).astype(BF16)).astype(BF16)

    settle(landed.at[pl.ds(0, others)], spread_r)
    settle(spread.at[pl.ds(0, others)], spread_s)
    for g in range(3):
        own[:, g * third : (g + 1) * third] = mm(from_wire[g], landed[...]).astype(BF16)

    def ring(part, way, step):
        ahead = 1 - 2 * way
        block = (exp + exps - ahead * step) % exps
        return pltpu.make_async_remote_copy(
            src_ref=every.at[part, block], dst_ref=every.at[part, block],
            send_sem=every_s.at[part], recv_sem=every_r.at[part, way, step],
            device_id={"exp": (exp + exps + ahead) % exps}, device_id_type=MESH)

    def ring_wait(part, way, step):
        block = (exp + exps - (1 - 2 * way) * (step + 1)) % exps
        view = every.at[part, block]
        pltpu.make_async_copy(view, view, every_r.at[part, way, step]).wait()

    half = exps // 2
    for wave in range(parts + half):
        part = wave - half
        if part >= 0:
            for way in range(2):
                ring_wait(part, way, half - 1 - (part + way) % 2)
            rows = every[part].reshape(exps * group, width)
            leave[part] = mm(pick, rows).astype(BF16)

            @pl.loop(1, seqs)
            def _(p):
                slots(leave, arrive, part, plane(p), seq, leave_s, leave_r).start()

            arrive[part, mine] = leave[part, mine]
        for part in range(parts):
            step = wave - part
            for way in range(2):
                if 0 <= step < half - (part + way) % 2:
                    if step == 0 and way == 0:
                        every[part, exp] = own[part * group : part * group + group]
                    if step:
                        ring_wait(part, way, step - 1)
                    ring(part, way, step).start()

    load_up.wait()
    load_down.wait()

    def send_back(part, piece, peer, start, size):
        cols = pl.ds(start, size)
        return pltpu.make_async_remote_copy(
            src_ref=back.at[part, pl.ds(pl.multiple_of(peer * 16, 16), 16), cols],
            dst_ref=home.at[part, mine, cols], send_sem=back_s.at[part], recv_sem=back_r.at[part + piece],
            device_id={"seq": peer}, device_id_type=MESH)

    def run_expert(part, pieces):
        settle(arrive.at[part, pl.ds(0, others)], leave_r.at[part])
        score = 1.0 / (1.0 + jnp.exp(-mm(arrive[part], router_col)))

        @pl.loop(0, hidden_width // 256)
        def _(j):
            rows = arrive[part]
            left = mm(rows, wgu[:, pl.ds(pl.multiple_of(j * 256, 256), 256)])
            right = mm(rows, wgu[:, pl.ds(pl.multiple_of(hidden_width + j * 256, 256), 256)])
            inner[:, pl.ds(pl.multiple_of(j * 256, 256), 256)] = (left / (1.0 + jnp.exp(-left)) * right).astype(BF16)

        weight = jnp.concatenate([score] * 3, axis=1)
        for g in range(3):
            cols = pl.ds(g * third, third)
            back[part, :, cols] = (weight * mm(inner[...], wd[:, cols])).astype(BF16)
        for piece, (start, size) in enumerate(pieces):

            @pl.loop(1, seqs)
            def _(p):
                send_back(part, piece, plane(p), start, size).start()

        home[part, mine] = back[part, mine]

    def deliver(part, piece, peer, start, size):
        cols = pl.ds(start, size)
        return pltpu.make_async_remote_copy(
            src_ref=give.at[part, peer, :, cols], dst_ref=take.at[part, exp, :, cols],
            send_sem=give_s.at[part], recv_sem=give_r.at[part + piece], device_id={"exp": peer}, device_id_type=MESH)

    def hand_over(part, pieces):
        for piece, (start, size) in enumerate(pieces):
            cols = pl.ds(start, size)
            settle(home.at[part, pl.ds(0, others), cols], back_r.at[part + piece])
            give[part, :, :, cols] = mm(unpick, home[part, :, cols]).astype(BF16).reshape(exps, group, size)

            @pl.loop(1, exps)
            def _(d):
                deliver(part, piece, column(d), start, size).start()

        take[part, exp] = give[part, exp]

    def add_up(part, pieces):
        for piece, (start, size) in enumerate(pieces):
            settle(take.at[part, pl.ds(0, exps - 1), :, pl.ds(start, size)], give_r.at[part + piece])
        own_rows = pl.ds(pl.multiple_of(part * group, group), group)
        settle(every.at[part, pl.ds(0, exps - 1)], every_s.at[part])
        total = take[part, 0].astype(F32)
        for c in range(1, exps):
            total = total + take[part, c].astype(F32)
        own[own_rows] = total.astype(BF16)

    whole = ((0, width),)
    split_last = ((0, 2 * third), (2 * third, third))
    for stage in (run_expert, hand_over, add_up):

        @pl.loop(0, parts - 1)
        def _(part):
            stage(part, whole)

        stage(parts - 1, split_last)

    lay_out(own[...])

    @pl.loop(1, seqs)
    def _(p):
        wire(plane(p), seq, final, end_s, end_r).start()

    final[mine] = spread[mine]
    settle(final.at[pl.ds(0, others)], end_r)
    scale = route_scale / denom
    for g in range(3):
        cols = pl.ds(g * third, third)
        out_ref[:, cols] = (hidden_ref[:, cols] + scale * mm(from_wire[g], final[...])).astype(BF16)
    settle(spread.at[pl.ds(0, others)], end_s)

    @pl.loop(0, parts)
    def _(part):
        settle(leave.at[part, pl.ds(0, others)], leave_s.at[part])
        settle(back.at[part, pl.ds(0, others)], back_s.at[part])
        settle(give.at[part, pl.ds(0, exps - 1)], give_s.at[part])


def experts(mb, q, o, gate, resid, gain, w_out, table, router, wgu, wd, seqs, exps):
    rows, width = resid.shape
    heads = mb.shape[0]
    parts, group = rows // seqs, seqs
    held = seqs * 16
    vmem = pl.BlockSpec(memory_space=pltpu.VMEM)
    hbm = pl.BlockSpec(memory_space=pl.ANY)
    dma = pltpu.SemaphoreType.DMA
    slots = pltpu.VMEM((parts, held, width), BF16)
    blocks = pltpu.VMEM((parts, exps, group, width), BF16)
    small = pltpu.VMEM((held, width // 3), BF16)
    mixes = pltpu.VMEM((exps, rows, heads * 128), BF16)
    return pl.pallas_call(
        expert_kernel,
        out_shape=jax.ShapeDtypeStruct((rows, width), BF16),
        in_specs=[vmem] + [hbm] * 4 + [vmem, hbm, vmem] + [hbm] * 3,
        out_specs=vmem,
        scratch_shapes=[
            pltpu.VMEM((rows, width), F32), pltpu.VMEM((rows, width), BF16), pltpu.VMEM(router.shape, BF16),
            pltpu.VMEM((NEAR, 128, 256), BF16), pltpu.VMEM((FAR, 128, 256), BF16),
            pltpu.VMEM((128, 256), BF16), pltpu.VMEM((2, 128, 128), BF16), mixes, mixes, pltpu.VMEM((2, exps, 128, width), BF16),
            pltpu.VMEM(q.shape, BF16), pltpu.VMEM(o.shape, F32), pltpu.VMEM(gate.shape, BF16),
            pltpu.VMEM(resid.shape, BF16),
            dma((2,)), dma((NEAR,)), dma((NEAR,)), dma((FAR,)), dma((FAR,)), dma((exps,)), dma((exps,)), dma((5,)), dma, dma, dma, dma((2, exps // 2)),
            small, small, small, pltpu.VMEM((rows, width), BF16),
            blocks, slots, slots, pltpu.VMEM((held, wd.shape[0]), BF16), slots, slots, blocks, blocks,
            pltpu.VMEM(wgu.shape, BF16), pltpu.VMEM(wd.shape, BF16),
            dma((3,)), dma, dma, dma((parts,)), dma((parts, 2, exps // 2)), dma((parts,)), dma((parts,)),
            dma((parts,)), dma((parts + 1,)), dma((parts,)), dma((parts + 1,)), dma, dma,
        ],
        compiler_params=pltpu.CompilerParams(
            collective_id=0, has_side_effects=True, vmem_limit_bytes=58 * 2**20
        ),
        name="mix_and_experts",
    )(mb, q, o, gate, resid, gain, w_out, table, router, wgu, wd)


def local(
    queries,
    keys,
    values,
    out_gate,
    decay_log,
    beta,
    w_out,
    resid,
    norm_gain,
    router,
    w_gate_up,
    w_down,
    block_experts,
):
    seq_count = lax.axis_size("seq")
    exp_count = lax.axis_size("exp")
    q_lead, o_lead, carried = delta(queries, keys, values, decay_log, beta)
    return experts(
        carried, q_lead, o_lead, out_gate, resid, norm_gain, w_out,
        block_experts.T, router, w_gate_up[0], w_down[0], seq_count, exp_count,
    )


def solution(mesh):
    return jax.shard_map(
        local,
        mesh=mesh,
        in_specs=(
            P("seq", "exp"),
            P("seq", "exp"),
            P("seq", "exp"),
            P("seq", "exp"),
            P("seq", "exp"),
            P("exp", "seq"),
            P("exp", None),
            P(("seq", "exp"), None),
            P(),
            P(),
            P(("seq", "exp"), None, None),
            P(("seq", "exp"), None, None),
            P(),
        ),
        out_specs=P(("seq", "exp"), None),
        check_vma=False,
    )
```

```python
import functools

import jax
import jax.numpy as jnp
from jax import lax
from jax.experimental import pallas as pl
from jax.experimental.pallas import tpu as pltpu
from jax.sharding import PartitionSpec as P

DK = 128
TOPK = 8
CH = 64
PAIR = 128
STEP = 512
NEAR = 8
FAR = 4
F32, BF16 = jnp.float32, jnp.bfloat16
MESH = pl.DeviceIdType.MESH
NN = (((1,), (0,)), ((), ()))
NT = (((1,), (1,)), ((), ()))
TN = (((0,), (0,)), ((), ()))

route_scale = 2.446
epsilon = 1e-06


def split(a):
    high = a.astype(BF16)
    return high, (a - high.astype(F32)).astype(BF16)


def mm(a, b, dims=NN):
    return lax.dot_general(a, b, dims, preferred_element_type=F32)


def dot1(a, b, dims=NN):
    return mm(a.astype(BF16), b.astype(BF16), dims)


def dot3(a, b, dims=NN):
    ah, al = split(a)
    bh, bl = split(b)
    return mm(ah, bh, dims) + (mm(ah, bl, dims) + mm(al, bh, dims))


def unit(x):
    return x * lax.rsqrt(jnp.sum(x * x, axis=-1, keepdims=True) + epsilon)


def delta_kernel(q_ref, k_ref, v_ref, d_ref, b_ref, qo_ref, oo_ref, mb_ref, state):
    heads = q_ref.shape[1] // 128
    step = pl.program_id(0)
    row = lax.broadcasted_iota(jnp.int32, (PAIR, PAIR), 0)
    col = lax.broadcasted_iota(jnp.int32, (PAIR, PAIR), 1)

    @pl.when(step == 0)
    def _():
        eye = jnp.where(row == col, 1.0, 0.0).astype(F32)
        for h in range(heads):
            state[h, :, :128] = eye
            state[h, :, 128:] = jnp.zeros((128, 128), F32)

    same = (row // CH) == (col // CH)
    incl = same & (col <= row)
    strict = same & (col < row)
    tri = jnp.where(incl, 1.0, 0.0).astype(BF16)
    eye = jnp.where(row == col, 1.0, 0.0).astype(F32)
    first = (row // 2) == (col // 2)
    masks = []
    size = 2
    while size < CH:
        level = ((row // (2 * size)) == (col // (2 * size))) & ((row // size) != (col // size))
        masks.append(jnp.where(level, 1.0, 0.0).astype(BF16))
        size *= 2
    pad = jnp.zeros((8 - heads, STEP), F32)
    betas = jnp.transpose(jnp.concatenate([b_ref[...], pad], axis=0))
    work = {}
    for p in range(STEP // PAIR):
        rows = pl.ds(p * PAIR, PAIR)
        log = d_ref[rows, :]
        l1 = log.astype(BF16)
        r1 = log - l1.astype(F32)
        l2 = r1.astype(BF16)
        l3 = (r1 - l2.astype(F32)).astype(BF16)
        acc = mm(tri, l1) + (mm(tri, l2) + mm(tri, l3))
        top = lax.broadcasted_iota(jnp.int32, acc.shape, 0) < CH
        last = jnp.where(top, acc[CH - 1 : CH, :], acc[PAIR - 1 : PAIR, :])
        grow = jnp.exp(acc)
        shrink = jnp.exp(-acc)
        tail = jnp.exp(last - acc)
        total = jnp.exp(last)
        for h in range(heads):
            cols = pl.ds(h * 128, 128)
            hs = slice(h * 128, h * 128 + 128)
            key = unit(k_ref[rows, cols].astype(F32))
            query = unit(q_ref[rows, cols].astype(F32))
            beta = betas[p * PAIR : p * PAIR + PAIR, h : h + 1]
            key_hat = key * grow[:, hs]
            key_inv = key * shrink[:, hs]
            key_end = key * tail[:, hs]
            query_hat = query * grow[:, hs]
            low = jnp.where(strict, dot3(key_hat, key_inv, NT) * beta, 0.0)
            score = jnp.where(incl, dot1(query_hat, key_inv, NT), 0.0)
            right = jnp.concatenate([beta * key_hat, beta * v_ref[rows, cols].astype(F32)], axis=1)
            work[p, h] = (low, right, score, query_hat, key_end, total[:, hs])
    invs = {at: eye - jnp.where(first, work[at][0], 0.0) for at in work}
    parts = {at: work[at][0].astype(BF16) for at in work}
    for mask in masks:
        held = {at: invs[at].astype(BF16) for at in work}
        steps = {at: mm(parts[at] * mask, held[at]).astype(BF16) for at in work}
        for at in work:
            invs[at] = invs[at] - mm(held[at], steps[at])
    rest = {at: eye - invs[at] - dot3(work[at][0], invs[at]) for at in work}
    for at in work:
        invs[at] = invs[at] + dot1(invs[at], rest[at])
    for at in work:
        work[at] = (dot3(invs[at], work[at][1]),) + work[at][2:]
    zero = jnp.zeros((CH, 128), F32)
    cur = [state[h] for h in range(heads)]
    for p in range(STEP // PAIR):
        for half in range(2):
            rs = slice(half * CH, half * CH + CH)
            at = pl.ds(p * PAIR + half * CH, CH)
            leads = []
            for h in range(heads):
                solved, score, query_hat, key_end, total = work[p, h]
                leads.append(dot3(jnp.concatenate([solved[rs, :128], query_hat[rs]], axis=0), cur[h]))
            for h in range(heads):
                solved, score, query_hat, key_end, total = work[p, h]
                upd = jnp.concatenate([zero, solved[rs, 128:]], axis=1) - leads[h][:CH]
                fade = jnp.transpose(total[half * CH : half * CH + 8, :])[:, :1]
                cur[h] = fade * cur[h] + dot3(key_end[rs], upd, TN)
                out = leads[h][CH:] + dot1(score[rs, rs], upd)
                qo_ref[at, h * 128 : h * 128 + 128] = out[:, :128].astype(qo_ref.dtype)
                oo_ref[at, h * 128 : h * 128 + 128] = out[:, 128:]
    for h in range(heads):
        state[h] = cur[h]

    @pl.when(step == pl.num_programs(0) - 1)
    def _():
        for h in range(heads):
            mb_ref[h] = state[h].astype(mb_ref.dtype)


def delta(q, k, v, d, bt):
    rows, width = q.shape
    heads = width // 128
    spec = pl.BlockSpec((STEP, width), lambda i: (i, 0))
    return pl.pallas_call(
        delta_kernel,
        grid=(rows // STEP,),
        out_shape=(
            jax.ShapeDtypeStruct((rows, width), BF16),
            jax.ShapeDtypeStruct((rows, width), F32),
            jax.ShapeDtypeStruct((heads, 128, 256), BF16),
        ),
        in_specs=[spec, spec, spec, spec, pl.BlockSpec((heads, STEP), lambda i: (0, i))],
        out_specs=(spec, spec, pl.BlockSpec((heads, 128, 256), lambda i: (0, 0, 0))),
        scratch_shapes=[pltpu.VMEM((heads, 128, 256), F32)],
        compiler_params=pltpu.CompilerParams(vmem_limit_bytes=60 * 2**20),
        cost_estimate=pl.CostEstimate(flops=5_000_000_000, bytes_accessed=6_000_000, transcendentals=0),
        name="delta_chunks",
    )(q, k, v, d, bt)


def mixer_stage(
    mb_ref, q_any, o_any, gate_any, resid_any, gain_ref, w_any, hidden_ref, normed_ref,
    near, far, total, enter, mixed, mix, wide, q_ref, o_ref, gate_ref, resid_ref,
    enter_s, near_s, near_r, far_s, far_r, mix_s, mix_r, fetch_s, share_s, share_r, ring_s, ring_r, later,
):
    heads = mb_ref.shape[0]
    seq, exp = lax.axis_index("seq"), lax.axis_index("exp")
    group, slot, core = seq // NEAR, seq % NEAR, seq % 2
    exps = mix.shape[0]
    rows = normed_ref.shape[0]
    pairs = ((w_any.at[pl.ds(pl.multiple_of(core * 128, 128), 128)], wide.at[core, exp]), (q_any, q_ref), (o_any, o_ref), (gate_any, gate_ref), (resid_any, resid_ref))
    fetches = [pltpu.make_async_copy(source, kept, fetch_s.at[i]) for i, (source, kept) in enumerate(pairs)]
    for fetch in fetches:
        fetch.start()

    reach = (exps // 2, exps // 2 - 1)

    def w_copy(way, step):
        ahead = 1 - 2 * way
        view = wide.at[core, (exp + exps - ahead * step) % exps]
        return pltpu.make_async_remote_copy(
            src_ref=view, dst_ref=view, send_sem=ring_s, recv_sem=ring_r.at[way, step],
            device_id={"exp": (exp + exps + ahead) % exps}, device_id_type=MESH)

    def share(block):
        view = wide.at[core, block]
        pltpu.make_async_remote_copy(
            src_ref=view, dst_ref=view, send_sem=share_s, recv_sem=share_r,
            device_id={"seq": seq + 1 - 2 * core}, device_id_type=MESH).start()

    def advance(step):
        for way in range(2):
            if step <= reach[way]:
                block = (exp + exps - (1 - 2 * way) * step) % exps
                view = wide.at[core, block]
                pltpu.make_async_copy(view, view, ring_r.at[way, step - 1]).wait()
                if step < reach[way]:
                    w_copy(way, step).start()
                share(block)

    def near_copy(peer, place):
        return pltpu.make_async_remote_copy(
            src_ref=mb_ref.at[peer % 2], dst_ref=near.at[place], send_sem=near_s.at[peer], recv_sem=near_r.at[place],
            device_id={"seq": group * NEAR + peer}, device_id_type=MESH)

    def far_copy(peer, place):
        return pltpu.make_async_remote_copy(
            src_ref=total, dst_ref=far.at[place], send_sem=far_s.at[peer], recv_sem=far_r.at[place],
            device_id={"seq": peer * NEAR + slot}, device_id_type=MESH)

    def mix_copy(peer, place):
        return pltpu.make_async_remote_copy(
            src_ref=mixed.at[peer], dst_ref=mix.at[place], send_sem=mix_s.at[peer], recv_sem=mix_r.at[place],
            device_id={"exp": peer}, device_id_type=MESH)

    for d in range(1, NEAR):
        near_copy((slot + d) % NEAR, slot).start()
    near[slot] = mb_ref[core]
    for fetch in fetches:
        fetch.wait()
    w_copy(0, 0).start()
    w_copy(1, 0).start()
    share(exp)
    for fetch in later:
        fetch.start()
    row = lax.broadcasted_iota(jnp.int32, (128, 256), 0)
    col = lax.broadcasted_iota(jnp.int32, (128, 256), 1)
    start = jnp.where(row == col, 1.0, 0.0).astype(F32)
    shifts = col >= 128

    def apply(block, carried):
        high, low = split(carried)
        lead = block[:, :128]
        return mm(lead, high) + mm(lead, low)

    cur, even, odd = start, start, start
    for j in range(NEAR):
        @pl.when(j != slot)
        def _():
            near_copy(j, j).wait_recv()

        if j % 2:
            odd = jnp.where(slot // 2 == j // 2, cur, odd)
        else:
            even = jnp.where(slot // 2 == j // 2, cur, even)
        block = near[j]
        cur = apply(block, cur) + jnp.where(shifts, block.astype(F32), 0.0)
    total[...] = cur.astype(BF16)
    for d in range(1, FAR):
        far_copy((group + d) % FAR, group).start()
    far[group] = total[...]
    advance(1)
    state = jnp.zeros((128, 128), F32)
    for g in range(FAR):
        @pl.when(g != group)
        def _():
            far_copy(g, g).wait_recv()

        block = far[g]
        state = jnp.where(g < group, apply(block, state) + block[:, 128:].astype(F32), state)
    first = dot3(even[:, :128], state) + even[:, 128:]
    second = dot3(odd[:, :128], state) + odd[:, 128:]
    enter[0] = jnp.where(core == 0, second, first).astype(BF16)
    hand = pltpu.make_async_remote_copy(
        src_ref=enter.at[0], dst_ref=enter.at[1], send_sem=enter_s.at[0], recv_sem=enter_s.at[1],
        device_id={"seq": seq + 1 - 2 * core}, device_id_type=MESH)
    hand.start()
    advance(2)
    mine = jnp.where(core == 0, first, second)
    hand.wait()
    theirs = enter[1].astype(F32)
    parts = [split(jnp.where(core == h, mine, theirs)) for h in range(heads)]

    def mix_rows(peer):
        at = pl.ds(pl.multiple_of(peer * rows, rows), rows)
        for h in range(heads):
            cols = pl.ds(h * 128, 128)
            query = q_ref[at, cols]
            out = mm(query, parts[h][0]) + mm(query, parts[h][1]) + o_ref[at, cols]
            out = out * lax.rsqrt(jnp.mean(out * out, axis=-1, keepdims=True) + epsilon)
            gate = gate_ref[at, cols].astype(F32)
            mixed[peer, :, cols] = (out / (1.0 + jnp.exp(-gate))).astype(BF16)

    for d in range(1, exps):
        peer = (exp + d) % exps
        mix_rows(peer)
        mix_copy(peer, exp).start()
        if d == exps // 2:
            advance(3)
    mix_rows(exp)
    mix[exp] = mixed[exp]
    advance(4)
    pltpu.make_async_copy(wide.at[1 - core], wide.at[1 - core], share_r).wait()
    acc = resid_ref[...].astype(F32)
    for d in range(exps):
        source = (exp + exps - d) % exps
        if d:
            mix_copy(source, source).wait_recv()
        for h in range(heads):
            acc = acc + mm(mix[source, :, h * 128 : h * 128 + 128], wide[h, source])
    hidden_ref[...] = acc
    scale = lax.rsqrt(jnp.mean(acc * acc, axis=-1, keepdims=True) + epsilon)
    normed_ref[...] = (acc * scale * gain_ref[...].reshape(1, -1)).astype(BF16)
    for d in range(1, NEAR):
        near_copy((slot + d) % NEAR, slot).wait_send()
    for d in range(1, FAR):
        far_copy((group + d) % FAR, group).wait_send()
    for d in range(1, exps):
        mix_copy((exp + d) % exps, exp).wait_send()
    pltpu.make_async_copy(wide.at[core], wide.at[core], share_s).wait()
    sent = wide.at[core, pl.ds(0, exps - 1)]
    pltpu.make_async_copy(sent, sent, ring_s).wait()


def expert_kernel(
    mb_ref, q_any, o_any, gate_any, resid_any, gain_ref, w_any, table_ref, router_any, wgu_ref, wd_ref, out_ref,
    hidden_ref, normed_ref, router_ref, near, far, total, enter, mixed, mix, wide, q_ref, o_ref, gate_ref, resid_ref,
    enter_s, near_s, near_r, far_s, far_r, mix_s, mix_r, mixer_s, share_s, share_r, ring_s, ring_r, spread, landed, final, own, every, leave, arrive, inner, back, home, give, take, wgu, wd,
    fetch_s, spread_s, spread_r, every_s, every_r, leave_s, leave_r, back_s, back_r, give_s, give_r, end_s, end_r,
):
    seq, exp = lax.axis_index("seq"), lax.axis_index("exp")
    seqs, exps = lax.axis_size("seq"), lax.axis_size("exp")
    width = out_ref.shape[1]
    third = width // 3
    parts = every.shape[0]
    group = every.shape[2]
    hidden_width = wd.shape[0]
    core, across, along = seq % 2, (seq // 2) % 4, seq // 8
    load_up = pltpu.make_async_copy(wgu_ref, wgu, fetch_s.at[0])
    load_down = pltpu.make_async_copy(wd_ref, wd, fetch_s.at[1])
    load_router = pltpu.make_async_copy(router_any, router_ref, fetch_s.at[2])

    def plane(p):
        step = p % 16
        turn = 1 + 2 * core
        dx = (step % 4) * turn
        dy = ((step // 4 + step) % 4) * turn
        return ((along + dy) % 4) * 8 + ((across + dx) % 4) * 2 + (core + p // 16) % 2

    def column(d):
        return (exp + d) % exps

    barrier = pltpu.get_barrier_semaphore()

    @pl.loop(1, seqs)
    def _(p):
        pl.semaphore_signal(barrier, inc=1, device_id={"seq": plane(p)}, device_id_type=MESH)

    @pl.loop(1, exps)
    def _(d):
        pl.semaphore_signal(barrier, inc=1, device_id={"exp": column(d)}, device_id_type=MESH)

    pl.semaphore_wait(barrier, seqs + exps - 2)
    mixer_stage(
        mb_ref, q_any, o_any, gate_any, resid_any, gain_ref, w_any, hidden_ref, normed_ref,
        near, far, total, enter, mixed, mix, wide, q_ref, o_ref, gate_ref, resid_ref,
        enter_s, near_s, near_r, far_s, far_r, mix_s, mix_r, mixer_s, share_s, share_r, ring_s, ring_r, (load_router, load_up, load_down))

    row = lax.broadcasted_iota(jnp.int32, (512, 128), 0)
    col = lax.broadcasted_iota(jnp.int32, (512, 128), 1)
    place = (row % 16) // 4 * 32 + row // 16 == col
    to_wire = [jnp.where(place & (row % 4 == g), 1.0, 0.0).astype(BF16) for g in range(3)]
    row = lax.broadcasted_iota(jnp.int32, (128, 512), 0)
    col = lax.broadcasted_iota(jnp.int32, (128, 512), 1)
    place = (col % 16) // 4 * 32 + col // 16 == row
    from_wire = [jnp.where(place & (col % 4 == g), 1.0, 0.0).astype(BF16) for g in range(3)]

    def lay_out(rows):
        total = mm(to_wire[0], rows[:, :third])
        total = total + mm(to_wire[1], rows[:, third : 2 * third])
        total = total + mm(to_wire[2], rows[:, 2 * third :])
        spread[...] = total.astype(BF16)

    def wire(peer, place, target, send, recv):
        return pltpu.make_async_remote_copy(
            src_ref=spread.at[pl.ds(pl.multiple_of(peer * 16, 16), 16)],
            dst_ref=target.at[pl.ds(pl.multiple_of(place * 16, 16), 16)],
            send_sem=send, recv_sem=recv, device_id={"seq": peer}, device_id_type=MESH)

    def slots(source, target, part, peer, place, send, recv):
        return pltpu.make_async_remote_copy(
            src_ref=source.at[part, pl.ds(pl.multiple_of(peer * 16, 16), 16)],
            dst_ref=target.at[part, pl.ds(pl.multiple_of(place * 16, 16), 16)],
            send_sem=send.at[part], recv_sem=recv.at[part], device_id={"seq": peer}, device_id_type=MESH)

    def settle(view, sem):
        pltpu.make_async_copy(view, view, sem).wait()

    others = (seqs - 1) * 16
    mine = pl.ds(pl.multiple_of(seq * 16, 16), 16)

    lay_out(normed_ref[...])

    @pl.loop(1, seqs)
    def _(p):
        wire(plane(p), seq, landed, spread_s, spread_r).start()

    landed[mine] = spread[mine]

    load_router.wait()
    count = table_ref.shape[1]
    row = lax.broadcasted_iota(jnp.int32, (count, count), 0)
    col = lax.broadcasted_iota(jnp.int32, (count, count), 1)
    order = jnp.where(row == (col % seqs) * exps + col // seqs, 1.0, 0.0).astype(BF16)
    table = mm(table_ref[...].astype(F32).astype(BF16), order)
    lane = lax.broadcasted_iota(jnp.int32, table.shape, 1)
    sub = lax.broadcasted_iota(jnp.int32, table.shape, 0)
    target = jnp.floor(jnp.sum(jnp.where(sub == exp, table, 0.0), axis=0, keepdims=True) / exps)
    hits = lax.broadcasted_iota(jnp.int32, (seqs, 256), 0).astype(F32) == target
    before = lax.broadcasted_iota(jnp.int32, (256, 256), 0) < lax.broadcasted_iota(jnp.int32, (256, 256), 1)
    counts = mm(jnp.where(hits, 1.0, 0.0).astype(BF16), jnp.where(before, 1.0, 0.0).astype(BF16))
    rank = jnp.sum(jnp.where(hits, counts, 0.0), axis=0, keepdims=True)
    goal = target * 16.0 + rank
    pick = jnp.where(lax.broadcasted_iota(jnp.int32, (512, 256), 0).astype(F32) == goal, 1.0, 0.0)
    unpick = jnp.transpose(pick).astype(BF16)
    pick = pick.astype(BF16)
    ids = jnp.sum(jnp.where(lane == exp * seqs + seq, table, 0.0), axis=1, keepdims=True)
    chosen = jnp.sum(jnp.where(lane.astype(F32) == ids, 1.0, 0.0), axis=0, keepdims=True)
    scores = mm(normed_ref[...], router_ref[...])
    denom = jnp.sum(chosen / (1.0 + jnp.exp(-scores)), axis=1, keepdims=True)
    here = lax.broadcasted_iota(jnp.int32, (256, 128), 0) == seq * exps + exp
    router_col = mm(router_ref[...], jnp.where(here, 1.0, 0.0).astype(BF16)).astype(BF16)

    settle(landed.at[pl.ds(0, others)], spread_r)
    settle(spread.at[pl.ds(0, others)], spread_s)
    for g in range(3):
        own[:, g * third : (g + 1) * third] = mm(from_wire[g], landed[...]).astype(BF16)

    def ring(part, way, step):
        ahead = 1 - 2 * way
        block = (exp + exps - ahead * step) % exps
        return pltpu.make_async_remote_copy(
            src_ref=every.at[part, block], dst_ref=every.at[part, block],
            send_sem=every_s.at[part], recv_sem=every_r.at[part, way, step],
            device_id={"exp": (exp + exps + ahead) % exps}, device_id_type=MESH)

    def ring_wait(part, way, step):
        block = (exp + exps - (1 - 2 * way) * (step + 1)) % exps
        view = every.at[part, block]
        pltpu.make_async_copy(view, view, every_r.at[part, way, step]).wait()

    half = exps // 2
    for wave in range(parts + half):
        part = wave - half
        if part >= 0:
            for way in range(2):
                ring_wait(part, way, half - 1 - (part + way) % 2)
            rows = every[part].reshape(exps * group, width)
            leave[part] = mm(pick, rows).astype(BF16)

            @pl.loop(1, seqs)
            def _(p):
                slots(leave, arrive, part, plane(p), seq, leave_s, leave_r).start()

            arrive[part, mine] = leave[part, mine]
        for part in range(parts):
            step = wave - part
            for way in range(2):
                if 0 <= step < half - (part + way) % 2:
                    if step == 0 and way == 0:
                        every[part, exp] = own[part * group : part * group + group]
                    if step:
                        ring_wait(part, way, step - 1)
                    ring(part, way, step).start()

    load_up.wait()
    load_down.wait()

    def send_back(part, piece, peer, start, size):
        cols = pl.ds(start, size)
        return pltpu.make_async_remote_copy(
            src_ref=back.at[part, pl.ds(pl.multiple_of(peer * 16, 16), 16), cols],
            dst_ref=home.at[part, mine, cols], send_sem=back_s.at[part], recv_sem=back_r.at[part + piece],
            device_id={"seq": peer}, device_id_type=MESH)

    def run_expert(part, pieces):
        settle(arrive.at[part, pl.ds(0, others)], leave_r.at[part])
        score = 1.0 / (1.0 + jnp.exp(-mm(arrive[part], router_col)))

        @pl.loop(0, hidden_width // 256)
        def _(j):
            rows = arrive[part]
            left = mm(rows, wgu[:, pl.ds(pl.multiple_of(j * 256, 256), 256)])
            right = mm(rows, wgu[:, pl.ds(pl.multiple_of(hidden_width + j * 256, 256), 256)])
            inner[:, pl.ds(pl.multiple_of(j * 256, 256), 256)] = (left / (1.0 + jnp.exp(-left)) * right).astype(BF16)

        weight = jnp.concatenate([score] * 3, axis=1)
        for g in range(3):
            cols = pl.ds(g * third, third)
            back[part, :, cols] = (weight * mm(inner[...], wd[:, cols])).astype(BF16)
        for piece, (start, size) in enumerate(pieces):

            @pl.loop(1, seqs)
            def _(p):
                send_back(part, piece, plane(p), start, size).start()

        home[part, mine] = back[part, mine]

    def deliver(part, piece, peer, start, size):
        cols = pl.ds(start, size)
        return pltpu.make_async_remote_copy(
            src_ref=give.at[part, peer, :, cols], dst_ref=take.at[part, exp, :, cols],
            send_sem=give_s.at[part], recv_sem=give_r.at[part + piece], device_id={"exp": peer}, device_id_type=MESH)

    def hand_over(part, pieces):
        for piece, (start, size) in enumerate(pieces):
            cols = pl.ds(start, size)
            settle(home.at[part, pl.ds(0, others), cols], back_r.at[part + piece])
            give[part, :, :, cols] = mm(unpick, home[part, :, cols]).astype(BF16).reshape(exps, group, size)

            @pl.loop(1, exps)
            def _(d):
                deliver(part, piece, column(d), start, size).start()

        take[part, exp] = give[part, exp]

    def add_up(part, pieces):
        for piece, (start, size) in enumerate(pieces):
            settle(take.at[part, pl.ds(0, exps - 1), :, pl.ds(start, size)], give_r.at[part + piece])
        own_rows = pl.ds(pl.multiple_of(part * group, group), group)
        settle(every.at[part, pl.ds(0, exps - 1)], every_s.at[part])
        total = take[part, 0].astype(F32)
        for c in range(1, exps):
            total = total + take[part, c].astype(F32)
        own[own_rows] = total.astype(BF16)

    whole = ((0, width),)
    split_last = ((0, 2 * third), (2 * third, third - 128), (width - 128, 128))
    for stage in (run_expert, hand_over, add_up):

        @pl.loop(0, parts - 1)
        def _(part):
            stage(part, whole)

        stage(parts - 1, split_last)

    lay_out(own[...])

    @pl.loop(1, seqs)
    def _(p):
        wire(plane(p), seq, final, end_s, end_r).start()

    final[mine] = spread[mine]
    settle(final.at[pl.ds(0, others)], end_r)
    scale = route_scale / denom
    for g in range(3):
        cols = pl.ds(g * third, third)
        out_ref[:, cols] = (hidden_ref[:, cols] + scale * mm(from_wire[g], final[...])).astype(BF16)
    settle(spread.at[pl.ds(0, others)], end_s)

    @pl.loop(0, parts)
    def _(part):
        settle(leave.at[part, pl.ds(0, others)], leave_s.at[part])
        settle(back.at[part, pl.ds(0, others)], back_s.at[part])
        settle(give.at[part, pl.ds(0, exps - 1)], give_s.at[part])


def experts(mb, q, o, gate, resid, gain, w_out, table, router, wgu, wd, seqs, exps):
    rows, width = resid.shape
    heads = mb.shape[0]
    parts, group = rows // seqs, seqs
    held = seqs * 16
    vmem = pl.BlockSpec(memory_space=pltpu.VMEM)
    hbm = pl.BlockSpec(memory_space=pl.ANY)
    dma = pltpu.SemaphoreType.DMA
    slots = pltpu.VMEM((parts, held, width), BF16)
    blocks = pltpu.VMEM((parts, exps, group, width), BF16)
    small = pltpu.VMEM((held, width // 3), BF16)
    mixes = pltpu.VMEM((exps, rows, heads * 128), BF16)
    return pl.pallas_call(
        expert_kernel,
        out_shape=jax.ShapeDtypeStruct((rows, width), BF16),
        in_specs=[vmem] + [hbm] * 4 + [vmem, hbm, vmem] + [hbm] * 3,
        out_specs=vmem,
        scratch_shapes=[
            pltpu.VMEM((rows, width), F32), pltpu.VMEM((rows, width), BF16), pltpu.VMEM(router.shape, BF16),
            pltpu.VMEM((NEAR, 128, 256), BF16), pltpu.VMEM((FAR, 128, 256), BF16),
            pltpu.VMEM((128, 256), BF16), pltpu.VMEM((2, 128, 128), BF16), mixes, mixes, pltpu.VMEM((2, exps, 128, width), BF16),
            pltpu.VMEM(q.shape, BF16), pltpu.VMEM(o.shape, F32), pltpu.VMEM(gate.shape, BF16),
            pltpu.VMEM(resid.shape, BF16),
            dma((2,)), dma((NEAR,)), dma((NEAR,)), dma((FAR,)), dma((FAR,)), dma((exps,)), dma((exps,)), dma((5,)), dma, dma, dma, dma((2, exps // 2)),
            small, small, small, pltpu.VMEM((rows, width), BF16),
            blocks, slots, slots, pltpu.VMEM((held, wd.shape[0]), BF16), slots, slots, blocks, blocks,
            pltpu.VMEM(wgu.shape, BF16), pltpu.VMEM(wd.shape, BF16),
            dma((3,)), dma, dma, dma((parts,)), dma((parts, 2, exps // 2)), dma((parts,)), dma((parts,)),
            dma((parts,)), dma((parts + 2,)), dma((parts,)), dma((parts + 2,)), dma, dma,
        ],
        compiler_params=pltpu.CompilerParams(
            collective_id=0, has_side_effects=True, vmem_limit_bytes=58 * 2**20
        ),
        name="mix_and_experts",
    )(mb, q, o, gate, resid, gain, w_out, table, router, wgu, wd)


def local(
    queries,
    keys,
    values,
    out_gate,
    decay_log,
    beta,
    w_out,
    resid,
    norm_gain,
    router,
    w_gate_up,
    w_down,
    block_experts,
):
    seq_count = lax.axis_size("seq")
    exp_count = lax.axis_size("exp")
    q_lead, o_lead, carried = delta(queries, keys, values, decay_log, beta)
    return experts(
        carried, q_lead, o_lead, out_gate, resid, norm_gain, w_out,
        block_experts.T, router, w_gate_up[0], w_down[0], seq_count, exp_count,
    )


def solution(mesh):
    return jax.shard_map(
        local,
        mesh=mesh,
        in_specs=(
            P("seq", "exp"),
            P("seq", "exp"),
            P("seq", "exp"),
            P("seq", "exp"),
            P("seq", "exp"),
            P("exp", "seq"),
            P("exp", None),
            P(("seq", "exp"), None),
            P(),
            P(),
            P(("seq", "exp"), None, None),
            P(("seq", "exp"), None, None),
            P(),
        ),
        out_specs=P(("seq", "exp"), None),
        check_vma=False,
    )
```
